512 devices in a mesh: group: 8 (over y_lo, core), dp: 64 (over x, y_hi, z).
Axes of the slice: x: 4, y: 8 (y_hi: 2, y_lo: 4; y = y_hi * 4 + y_lo), z: 8, core: 2. Of those that a mesh axis runs over, the one named last changes fastest.
Arguments:
- partials: bfloat16 [8, 64, 2, 384, 1024], P('group', 'dp'), as said below
- momentum: float32 [8, 2, 384, 1024], P('group', None, 'dp'), may hold values from -6 to 6
Outputs:
- update: bfloat16 [8, 2, 384, 1024], P('group')
- momentum_out: float32 [8, 2, 384, 1024], P('group', None, 'dp')
The draws below stay inside these ranges and needn't reach their ends.
Inputs may be any that keep to these rules, and one draw needn't show every extreme that they name: `partials`: each replica's gradient has row and column scales that differ.
All inputs are finite; a program needn't handle non-finite values.
Results may differ from the reference program's by a relative error of at most 0.023.
Values may be sent and summed in bfloat16 or wider, within the bound.
A program may use at most 64 MiB of HBM per device.

```python
import math
import jax
import jax.numpy as jnp
from jax import lax

MATS = 2
ROWS = 384
COLS = 1024
ITERS = 5
GROUPS = 8
PARTIALS = 64


def draw_partials(key, part):
    key = jax.random.fold_in(key, 11)
    key_base, key_rows, key_cols = jax.random.split(key, 3)
    shape = (GROUPS, PARTIALS, MATS, ROWS, COLS)
    row_top = math.log(10.0)
    base = jax.random.normal(key_base, shape, jnp.float32)
    row_scale = jnp.exp(jax.random.uniform(key_rows, (GROUPS, 1, MATS, ROWS, 1), jnp.float32, 0.0, row_top))
    col_scale = jnp.exp(jax.random.uniform(key_cols, (GROUPS, 1, MATS, 1, COLS), jnp.float32, 0.0, math.log(10.0)))
    row_ramp = jnp.exp(0.5 * math.log(3.0) * jnp.arange(ROWS, dtype=jnp.float32) / ROWS).reshape(1, 1, 1, ROWS, 1)
    group_ramp = jnp.exp(0.5 * math.log(3.0) * jnp.arange(GROUPS, dtype=jnp.float32) / max(GROUPS - 1, 1)).reshape(GROUPS, 1, 1, 1, 1)
    return (base * row_scale * col_scale * row_ramp * group_ramp).astype(jnp.bfloat16)


def steps_of(key, extent, cuts, least, top_value):
    gain = 1.0
    for axis_at, blocks in cuts:
        steps = jax.random.uniform(jax.random.fold_in(jax.random.fold_in(key, 6), axis_at), (blocks,), jnp.float32, least / len(cuts), top_value / len(cuts))
        gain = gain * jnp.repeat(jnp.exp(steps), extent[axis_at] // blocks).reshape((-1,) + (1,) * (len(extent) - 1 - axis_at))
    return gain


def bell_draw(key, shape, width, limit, pieces=(), held_as=jnp.bfloat16):
    values = jax.random.normal(key, shape, jnp.float32) * width
    if len(pieces) > 0:
        values = steps_of(key, shape, pieces, -0.22, 0.18) * values
    return jnp.clip(values, min=-limit, max=limit).astype(held_as)


def setup_inputs(seed: int = 0) -> dict:
    keys = jax.random.split(jax.random.key(seed), 3)
    return {
        "partials": draw_partials(jax.random.fold_in(keys[2], 71), 0),
        "momentum": bell_draw(keys[1], (GROUPS, MATS, ROWS, COLS), 1.0, 6.0, ((0, 8), (2, 64)), jnp.float32),
    }


decay_rate = 0.95
coef_a = 3.4445
coef_b = -4.775
coef_c = 2.0315

def newton_schulz(matrix):
    as_float = matrix.astype(jnp.float32)
    frob_norm = jnp.sqrt(jnp.sum(as_float * as_float))
    current = (as_float / (frob_norm + 1e-07)).astype(jnp.bfloat16)
    final_scale = 0.2 * math.sqrt(max(ROWS, COLS))
    result = None
    for iteration in range(ITERS):
        gram_matrix = jnp.dot(current, current.T, preferred_element_type=jnp.float32).astype(jnp.bfloat16)
        gram_square = jnp.dot(gram_matrix, gram_matrix, preferred_element_type=jnp.float32)
        mixed_poly = (coef_b * gram_matrix.astype(jnp.float32) + coef_c * gram_square).astype(jnp.bfloat16)
        stepped = coef_a * current.astype(jnp.float32) + jnp.dot(mixed_poly, current, preferred_element_type=jnp.float32)
        if iteration + 1 < ITERS:
            current = stepped.astype(jnp.bfloat16)
        else:
            result = (stepped * final_scale).astype(jnp.bfloat16)
    return result

def reference(partials, momentum):
    summed = lax.optimization_barrier(jnp.sum(partials, axis=1, dtype=jnp.float32))
    square_sum = jnp.sum(summed * summed)
    entries = GROUPS * MATS * ROWS * COLS
    clip_factor = jnp.minimum(1.0, math.sqrt(entries) / jnp.sqrt(square_sum + 1e-06))
    grad = clip_factor * summed
    momentum_out = decay_rate * momentum + grad
    blended = (grad + decay_rate * momentum_out).astype(jnp.bfloat16)
    flat = blended.reshape(GROUPS * MATS, ROWS, COLS)
    update = lax.map(newton_schulz, flat).reshape(GROUPS, MATS, ROWS, COLS)
    return (update, momentum_out)
```

```python
import functools
import math

import jax
import jax.numpy as jnp
from jax import lax
from jax.experimental import pallas as pl
from jax.experimental.pallas import tpu as pltpu
from jax.sharding import PartitionSpec as P

MESH = pl.DeviceIdType.MESH

MATS = 2
ROWS = 384
COLS = 1024
ITERS = 5
GROUPS = 8

NX, NYH, NZ, NYL, NC = 4, 2, 8, 4, 2
SLAB = ROWS // (NX * NYH)
WIDE = COLS // NZ
TOP = SLAB * 2 // 3
REST = SLAB - TOP
OWN = SLAB // NZ
OWN_PAD = -(-OWN // 8) * 8

decay_rate = 0.95
coef_a = 3.4445
coef_b = -4.775
coef_c = 2.0315

bf16, f32 = jnp.bfloat16, jnp.float32


def place():
    d = lax.axis_index("dp")
    g = lax.axis_index("group")
    return d // (NYH * NZ), (d // NZ) % NYH, d % NZ, g // NC, g % NC


def dp_index(x, yh, z):
    return x * (NYH * NZ) + yh * NZ + z


def comm_kernel(p_ref, m_ref, xo_ref, own_a, own_b, got_a, got_b, sum_a, sum_b, got_a2, got_b2,
                m_out, m_got, q_out, q_got, lsem, ssem, rsem):
    x, yh, z, yl, core = place()
    counter = [0]

    def wrap(v, n):
        return lax.rem(v, n)

    def send(src, dst, device):
        i = counter[0]
        counter[0] += 1
        copy = pltpu.make_async_remote_copy(
            src_ref=src, dst_ref=dst, send_sem=ssem.at[i], recv_sem=rsem.at[i],
            device_id=device, device_id_type=MESH)
        copy.start()
        return copy

    x_peers = [(dx, 0) for dx in range(1, NX)]
    z_peers = list(range(1, NZ))
    yz_peers = [(dy, dz) for dy in range(NYH) for dz in range(NZ) if (dy, dz) != (0, 0)]
    xy_peers = [(dx, dy) for dx in range(NX) for dy in range(NYH) if (dx, dy) != (0, 0)]

    def at_z(dz):
        return {"dp": dp_index(x, yh, wrap(z + dz, NZ))}

    def at_yz(dy, dz):
        return {"dp": dp_index(x, wrap(yh + dy, NYH), wrap(z + dz, NZ))}

    def at_xy(dx, dy):
        return {"dp": dp_index(wrap(x + dx, NX), wrap(yh + dy, NYH), z)}

    def at_xc(dx, dc):
        return {"group": yl * NC + wrap(core + dc, NC), "dp": dp_index(wrap(x + dx, NX), yh, z)}

    def at_y(dy):
        y = wrap(yh * NYL + yl + dy, NYH * NYL)
        return {"group": lax.rem(y, NYL) * NC + core, "dp": dp_index(x, y // NYL, z)}

    xc_peers = [(dx, dc) for dx in range(NX) for dc in range(NC) if (dx, dc) != (0, 0)]
    y_peers = list(range(1, NYH * NYL))

    own_cols = pl.ds(pl.multiple_of(z * WIDE, WIDE), WIDE)

    def cols_of(zz):
        return pl.ds(pl.multiple_of(zz * WIDE, WIDE), WIDE)

    local_a = pltpu.make_async_copy(p_ref.at[:, x, :, 0:TOP, :], own_a, lsem.at[0])
    local_b = pltpu.make_async_copy(p_ref.at[:, :, :, TOP:SLAB, own_cols], own_b, lsem.at[1])
    local_a.start()
    local_b.start()

    targets = [at_yz(dy, dz) for dy, dz in yz_peers] + [at_xy(dx, dy) for dx, dy in xy_peers if dx != 0]
    targets += [at_xc(dx, dc) for dx, dc in xc_peers if dc != 0]
    targets += [at_y(dy) for dy in y_peers if dy % NYL != 0]
    barrier = pltpu.get_barrier_semaphore()
    for device in targets:
        pl.semaphore_signal(barrier, inc=1, device_id=device, device_id_type=MESH)
    m_out[...] = jnp.zeros_like(m_out)
    m_out[:, 0:OWN, :] = m_ref[...]
    pl.semaphore_wait(barrier, len(targets))

    sends = []
    a1 = [[], []]
    b1 = []
    b_order = list(z_peers)
    for m in range(MATS):
        for dx, _ in x_peers:
            a1[m].append(send(p_ref.at[m, wrap(x + dx, NX), :, 0:TOP, :], got_a.at[m, dx - 1], at_xy(dx, 0)))
            if b_order:
                dz = b_order.pop(0)
                b1.append(send(p_ref.at[:, :, :, TOP:SLAB, cols_of(wrap(z + dz, NZ))], got_b.at[dz - 1], at_z(dz)))
    while b_order:
        dz = b_order.pop(0)
        b1.append(send(p_ref.at[:, :, :, TOP:SLAB, cols_of(wrap(z + dz, NZ))], got_b.at[dz - 1], at_z(dz)))
    m1 = [send(m_out.at[:, :, cols_of(wrap(z + dz, NZ))], m_got.at[wrap(z, NZ)], at_z(dz)) for dz in z_peers]
    m_got[z] = m_out[:, :, own_cols]
    local_a.wait()
    local_b.wait()

    for m in range(MATS):
        for copy in a1[m]:
            copy.wait_recv()
        total = own_a[m].astype(f32)
        for j in range(NX - 1):
            total = total + got_a[m, j].astype(f32)
        sum_a[m] = total.astype(bf16)
    a2 = [send(sum_a.at[:, wrap(yh + dy, NYH), :, cols_of(wrap(z + dz, NZ))], got_a2.at[j], at_yz(dy, dz))
          for j, (dy, dz) in enumerate(yz_peers)]
    for copy in b1:
        copy.wait_recv()
    total = own_b[...].astype(f32)
    for j in range(NZ - 1):
        total = total + got_b[j].astype(f32)
    sum_b[...] = total.astype(bf16)
    b2 = [send(sum_b.at[:, wrap(x + dx, NX), wrap(yh + dy, NYH)], got_b2.at[j], at_xy(dx, dy))
          for j, (dx, dy) in enumerate(xy_peers)]

    for copy in m1:
        copy.wait_recv()
    row = lax.broadcasted_iota(jnp.int32, (SLAB, NZ * OWN_PAD), 0)
    slot = lax.broadcasted_iota(jnp.int32, (SLAB, NZ * OWN_PAD), 1)
    pick = ((slot // OWN_PAD) * OWN + slot % OWN_PAD == row) & (slot % OWN_PAD < OWN)
    pick = pick.astype(f32)
    m_block = [jnp.dot(pick, m_got[:, m].reshape(NZ * OWN_PAD, WIDE), preferred_element_type=f32,
                       precision=lax.Precision.HIGHEST) for m in range(MATS)]

    for copy in a2:
        copy.wait_recv()
    top = sum_a[:, yh, :, own_cols].astype(f32)
    for j in range(len(yz_peers)):
        top = top + got_a2[j].astype(f32)
    for copy in b2:
        copy.wait_recv()
    rest = sum_b[:, x, yh].astype(f32)
    for j in range(len(xy_peers)):
        rest = rest + got_b2[j].astype(f32)

    square = jnp.zeros((8, WIDE), f32)
    for m in range(MATS):
        for part in (top[m], rest[m]):
            for r in range(0, part.shape[0], 8):
                square = square + part[r:r + 8] * part[r:r + 8]
    slot = 0
    q_sends = []
    for stage, (peers, at) in enumerate(((z_peers, at_z), (xc_peers, lambda t: at_xc(*t)), (y_peers, at_y))):
        q_out[stage] = square
        stage_sends = [send(q_out.at[stage], q_got.at[slot + j], at(peer)) for j, peer in enumerate(peers)]
        for j, copy in enumerate(stage_sends):
            copy.wait_recv()
            square = square + q_got[slot + j]
        slot += len(peers)
        q_sends += stage_sends
    square_sum = jnp.sum(jnp.sum(square, axis=1, keepdims=True), axis=0, keepdims=True)
    entries = GROUPS * MATS * ROWS * COLS
    clip = jnp.minimum(1.0, math.sqrt(entries) / jnp.sqrt(square_sum + 1e-06))

    for m in range(MATS):
        for part, lo in ((top[m], 0), (rest[m], TOP)):
            n = part.shape[0]
            grad = clip * part
            momentum_new = decay_rate * m_block[m][lo:lo + n] + grad
            xo_ref[m, x, yh, lo:lo + n, own_cols] = (grad + decay_rate * momentum_new).astype(bf16)
    block_a = xo_ref.at[:, x, yh, 0:TOP, own_cols]
    block_b = xo_ref.at[:, x, yh, TOP:SLAB, own_cols]
    a3 = [send(block_a, block_a, at_yz(dy, dz)) for dy, dz in yz_peers]
    b3 = [send(block_b, block_b, at_xy(dx, dy)) for dx, dy in xy_peers]
    for copy in a3:
        copy.wait_recv()
    a4 = []
    for m in range(MATS):
        strip = xo_ref.at[m, x, :, 0:TOP, :]
        a4 += [send(strip, strip, at_xy(dx, 0)) for dx, _ in x_peers]
    for copy in b3:
        copy.wait_recv()
    strip = xo_ref.at[:, :, :, TOP:SLAB, own_cols]
    b4 = [send(strip, strip, at_z(dz)) for dz in z_peers]
    for copy in a4 + b4:
        copy.wait_recv()
    for copy in a1[0] + a1[1] + b1 + m1 + a2 + b2 + q_sends + a3 + b3 + a4 + b4:
        copy.wait_send()


def comm(partials, momentum):
    n_q = (NZ - 1) + (NX * NC - 1) + (NYH * NYL - 1)
    n_copies = 2 * (MATS * (NX - 1) + (NZ - 1) + (NYH * NZ - 1) + (NX * NYH - 1)) + (NZ - 1) + n_q
    return pl.pallas_call(
        comm_kernel,
        name="reduce_blend_gather",
        out_shape=jax.ShapeDtypeStruct((MATS, NX, NYH, SLAB, COLS), bf16),
        in_specs=[pl.BlockSpec(memory_space=pl.ANY), pl.BlockSpec(memory_space=pltpu.VMEM)],
        out_specs=pl.BlockSpec(memory_space=pltpu.VMEM),
        scratch_shapes=[
            pltpu.VMEM((MATS, NYH, TOP, COLS), bf16),
            pltpu.VMEM((MATS, NX, NYH, REST, WIDE), bf16),
            pltpu.VMEM((MATS, NX - 1, NYH, TOP, COLS), bf16),
            pltpu.VMEM((NZ - 1, MATS, NX, NYH, REST, WIDE), bf16),
            pltpu.VMEM((MATS, NYH, TOP, COLS), bf16),
            pltpu.VMEM((MATS, NX, NYH, REST, WIDE), bf16),
            pltpu.VMEM((NYH * NZ - 1, MATS, TOP, WIDE), bf16),
            pltpu.VMEM((NX * NYH - 1, MATS, REST, WIDE), bf16),
            pltpu.VMEM((MATS, OWN_PAD, COLS), f32),
            pltpu.VMEM((NZ, MATS, OWN_PAD, WIDE), f32),
            pltpu.VMEM((3, 8, WIDE), f32),
            pltpu.VMEM((n_q, 8, WIDE), f32),
            pltpu.SemaphoreType.DMA((2,)),
            pltpu.SemaphoreType.DMA((n_copies,)),
            pltpu.SemaphoreType.DMA((n_copies,)),
        ],
        compiler_params=pltpu.CompilerParams(
            collective_id=0, has_side_effects=True, vmem_limit_bytes=32 << 20),
        cost_estimate=pl.CostEstimate(flops=10_000_000, bytes_accessed=8_000_000, transcendentals=0),
    )(partials, momentum)


def newton_kernel(x_ref, m_ref, u_ref, mo_ref, cur):
    x, yh, z, _, _ = place()
    final_scale = 0.2 * math.sqrt(max(ROWS, COLS))

    row = lax.broadcasted_iota(jnp.int32, (OWN_PAD, SLAB), 0)
    col = lax.broadcasted_iota(jnp.int32, (OWN_PAD, SLAB), 1)
    pick = ((col == z * OWN + row) & (row < OWN)).astype(f32).astype(bf16)
    for m in range(MATS):
        mine = jnp.dot(pick, x_ref[m, x, yh], preferred_element_type=f32)[0:OWN]
        old = m_ref[m]
        grad = (mine - (decay_rate * decay_rate) * old) * (1.0 / (1.0 + decay_rate))
        mo_ref[m] = decay_rate * old + grad

    for m in range(MATS):
        full = x_ref[m].reshape(ROWS, COLS).astype(f32)
        norm = jnp.sqrt(jnp.sum(jnp.sum(full * full, axis=1, keepdims=True), axis=0, keepdims=True))
        cur[m] = (full * (1.0 / (norm + 1e-07))).astype(bf16)

    def poly(m):
        here = cur[m]
        gram = lax.dot_general(here, here, (((1,), (1,)), ((), ())), preferred_element_type=f32).astype(bf16)
        square = jnp.dot(gram, gram, preferred_element_type=f32)
        return (coef_b * gram.astype(f32) + coef_c * square).astype(bf16)

    def step(_, carry):
        polys = [poly(m) for m in range(MATS)]
        for m in range(MATS):
            here = cur[m]
            cur[m] = (coef_a * here.astype(f32) + jnp.dot(polys[m], here, preferred_element_type=f32)).astype(bf16)
        return carry

    lax.fori_loop(0, ITERS - 1, step, 0)
    polys = [poly(m) for m in range(MATS)]
    for m in range(MATS):
        here = cur[m]
        last = coef_a * here.astype(f32) + jnp.dot(polys[m], here, preferred_element_type=f32)
        u_ref[m] = (last * final_scale).astype(bf16)


def newton(blended, momentum):
    vmem = pl.BlockSpec(memory_space=pltpu.VMEM)
    return pl.pallas_call(
        newton_kernel,
        name="newton_schulz",
        out_shape=(jax.ShapeDtypeStruct((MATS, ROWS, COLS), bf16), jax.ShapeDtypeStruct((MATS, OWN, COLS), f32)),
        in_specs=[vmem, vmem],
        out_specs=(vmem, vmem),
        scratch_shapes=[pltpu.VMEM((MATS, ROWS, COLS), bf16)],
        compiler_params=pltpu.CompilerParams(vmem_limit_bytes=40 << 20),
        cost_estimate=pl.CostEstimate(flops=7_200_000_000, bytes_accessed=3_200_000, transcendentals=0),
    )(blended, momentum)


def shards(partials, momentum):
    parts = partials.reshape(MATS, NX, NYH, SLAB, COLS)
    old = momentum.reshape(MATS, OWN, COLS)
    blended = comm(parts, old)
    update, momentum_out = newton(blended, old)
    return update[None], momentum_out[None]


def solution(mesh):
    in_specs = (P("group", "dp", None, None, None), P("group", None, "dp", None))
    out_specs = (P("group", None, None, None), P("group", None, "dp", None))
    return jax.shard_map(shards, mesh=mesh, in_specs=in_specs, out_specs=out_specs, check_vma=False)
```

```python
import functools
import math

import jax
import jax.numpy as jnp
from jax import lax
from jax.experimental import pallas as pl
from jax.experimental.pallas import tpu as pltpu
from jax.sharding import PartitionSpec as P

MESH = pl.DeviceIdType.MESH

MATS = 2
ROWS = 384
COLS = 1024
ITERS = 5
GROUPS = 8

NX, NYH, NZ, NYL, NC = 4, 2, 8, 4, 2
SLAB = ROWS // (NX * NYH)
WIDE = COLS // NZ
TOP = SLAB * 2 // 3
REST = SLAB - TOP
OWN = SLAB // NZ
OWN_PAD = -(-OWN // 8) * 8

decay_rate = 0.95
coef_a = 3.4445
coef_b = -4.775
coef_c = 2.0315

bf16, f32 = jnp.bfloat16, jnp.float32


def place():
    d = lax.axis_index("dp")
    g = lax.axis_index("group")
    return d // (NYH * NZ), (d // NZ) % NYH, d % NZ, g // NC, g % NC


def dp_index(x, yh, z):
    return x * (NYH * NZ) + yh * NZ + z


def comm_kernel(p_ref, m_ref, xo_ref, own_a, own_b, got_a, got_b, sum_a, sum_b, got_a2, got_b2,
                all_a, all_b, m_out, m_got, m_pair, m_a, m_b, q_got, lsem, ssem, rsem):
    x, yh, z, yl, core = place()
    counter = [0]

    def wrap(v, n):
        return lax.rem(v, n)

    sent = []

    def send(src, dst, device):
        i = counter[0]
        counter[0] += 1
        copy = pltpu.make_async_remote_copy(
            src_ref=src, dst_ref=dst, send_sem=ssem.at[i], recv_sem=rsem.at[i],
            device_id=device, device_id_type=MESH)
        copy.start()
        sent.append(copy)
        return copy

    x_peers = list(range(1, NX))
    z_peers = sorted(range(1, NZ), key=lambda d: -min(d, NZ - d))
    y_peers = list(range(1, NYH * NYL))
    yz_peers = [(dy, dz) for dy in range(NYH) for dz in range(NZ) if (dy, dz) != (0, 0)][::-1]
    xy_peers = [(dx, dy) for dx in range(NX) for dy in range(NYH) if (dx, dy) != (0, 0)][::-1]
    xc_peers = [(dx, dc) for dx in range(NX) for dc in range(NC) if (dx, dc) != (0, 0)]

    def at_z(dz):
        return {"dp": dp_index(x, yh, wrap(z + dz, NZ))}

    def at_x(dx):
        return {"dp": dp_index(wrap(x + dx, NX), yh, z)}

    def at_yz(t):
        return {"dp": dp_index(x, wrap(yh + t[0], NYH), wrap(z + t[1], NZ))}

    def at_xy(t):
        return {"dp": dp_index(wrap(x + t[0], NX), wrap(yh + t[1], NYH), z)}

    def at_xc(t):
        return {"group": yl * NC + wrap(core + t[1], NC), "dp": dp_index(wrap(x + t[0], NX), yh, z)}

    def at_y(dy):
        y = wrap(yh * NYL + yl + dy, NYH * NYL)
        return {"group": lax.rem(y, NYL) * NC + core, "dp": dp_index(x, y // NYL, z)}

    def cols_of(zz):
        return pl.ds(pl.multiple_of(zz * WIDE, WIDE), WIDE)

    own_cols = cols_of(z)

    local_a = pltpu.make_async_copy(p_ref.at[:, x, :, 0:TOP, :], own_a, lsem.at[0])
    local_b = pltpu.make_async_copy(p_ref.at[:, :, :, TOP:SLAB, own_cols], own_b, lsem.at[1])
    local_a.start()
    local_b.start()

    targets = [at_z(dz) for dz in z_peers] + [at_y(dy) for dy in y_peers] + [at_x(dx) for dx in x_peers]
    targets.append(at_xc((0, 1)))
    barrier = pltpu.get_barrier_semaphore()
    for device in targets:
        pl.semaphore_signal(barrier, inc=1, device_id=device, device_id_type=MESH)
    m_out[...] = jnp.zeros_like(m_out)
    for m in range(MATS):
        m_out[m, 0:OWN, :] = m_ref[:, m, :]
    m_got[z] = m_out[:, :, own_cols]
    pl.semaphore_wait(barrier, len(targets))

    m1 = [send(m_out.at[:, :, cols_of(wrap(z + dz, NZ))], m_got.at[z], at_z(dz)) for dz in z_peers]
    a1 = [[], []]
    b1 = []
    b_order = list(z_peers)

    def send_b():
        dz = b_order.pop(0)
        b1.append(send(p_ref.at[:, :, :, TOP:SLAB, cols_of(wrap(z + dz, NZ))], got_b.at[dz - 1], at_z(dz)))

    for m in range(MATS):
        for dx in x_peers:
            a1[m].append(send(p_ref.at[m, wrap(x + dx, NX), :, 0:TOP, :], got_a.at[m, dx - 1], at_x(dx)))
            if b_order:
                send_b()
    while b_order:
        send_b()

    row = lax.broadcasted_iota(jnp.int32, (SLAB, NZ * OWN_PAD), 0)
    slot = lax.broadcasted_iota(jnp.int32, (SLAB, NZ * OWN_PAD), 1)
    pick = ((slot // OWN_PAD) * OWN + slot % OWN_PAD == row) & (slot % OWN_PAD < OWN)
    pick = pick.astype(f32).astype(bf16)
    for copy in m1:
        copy.wait_recv()
    for m in range(MATS):
        block = jnp.dot(pick, m_got[:, m].reshape(NZ * OWN_PAD, WIDE).astype(bf16),
                        preferred_element_type=f32).astype(bf16)
        m_pair[m, yh] = block[0:TOP]
        m_b[m, x, yh] = block[TOP:SLAB]
    m2 = send(m_pair.at[:, yh], m_pair.at[:, yh], at_yz((1, 0)))

    local_a.wait()
    local_b.wait()
    for m in range(MATS):
        for copy in a1[m]:
            copy.wait_recv()
        total = own_a[m].astype(f32)
        for j in range(NX - 1):
            total = total + got_a[m, j].astype(f32)
        sum_a[m] = total.astype(bf16)
    a2 = [send(sum_a.at[:, wrap(yh + t[0], NYH), :, cols_of(wrap(z + t[1], NZ))], got_a2.at[j], at_yz(t))
          for j, t in enumerate(yz_peers)]
    for copy in b1:
        copy.wait_recv()
    total = own_b[...].astype(f32)
    for j in range(NZ - 1):
        total = total + got_b[j].astype(f32)
    sum_b[...] = total.astype(bf16)
    b2 = [send(sum_b.at[:, wrap(x + t[0], NX), wrap(yh + t[1], NYH)], got_b2.at[j], at_xy(t))
          for j, t in enumerate(xy_peers)]

    m4 = [send(m_b.at[:, x, yh], m_b.at[:, x, yh], at_xy(t)) for t in xy_peers]
    m2.wait_recv()
    m_a[:, :, :, own_cols] = m_pair[...]
    m3 = [send(m_pair, m_a.at[:, :, :, own_cols], at_z(dz)) for dz in z_peers]

    for copy in a2:
        copy.wait_recv()
    top = sum_a[:, yh, :, own_cols].astype(f32)
    for j in range(len(yz_peers)):
        top = top + got_a2[j].astype(f32)
    for copy in b2:
        copy.wait_recv()
    rest = sum_b[:, x, yh].astype(f32)
    for j in range(len(xy_peers)):
        rest = rest + got_b2[j].astype(f32)

    square = jnp.zeros((8, WIDE), f32)
    for m in range(MATS):
        for part in (top[m], rest[m]):
            for r in range(0, part.shape[0], 8):
                square = square + part[r:r + 8] * part[r:r + 8]

    def spread(stage, mine, peers, at):
        q_got[stage, mine] = square
        here = q_got.at[stage, mine]
        return [send(here, here, at(t)) for t in peers]

    def gather(stage, copies):
        for copy in copies:
            copy.wait_recv()
        total = q_got[stage, 0]
        for j in range(1, len(copies) + 1):
            total = total + q_got[stage, j]
        return total

    q = spread(0, z, z_peers, at_z)
    all_a[:, yh, :, own_cols] = top.astype(bf16)
    all_b[:, x, yh] = rest.astype(bf16)
    here = all_a.at[:, yh, :, own_cols]
    a3 = [send(here, here, at_yz(t)) for t in yz_peers]
    here = all_b.at[:, x, yh]
    b3 = [send(here, here, at_xy(t)) for t in xy_peers]
    square = gather(0, q)
    q = spread(1, x * NC + core, xc_peers, at_xc)
    square = gather(1, q)
    q = spread(2, yh * NYL + yl, y_peers, at_y)
    square = gather(2, q)
    square_sum = jnp.sum(jnp.sum(square, axis=1, keepdims=True), axis=0, keepdims=True)
    entries = GROUPS * MATS * ROWS * COLS
    clip = jnp.minimum(1.0, math.sqrt(entries) / jnp.sqrt(square_sum + 1e-06))
    scale = (1.0 + decay_rate) * clip

    for copy in m3 + a3:
        copy.wait_recv()
    a4 = []
    b4 = []
    for m in range(MATS):
        for j in range(NYH):
            xo_ref[m, x, j, 0:TOP, :] = (
                scale * all_a[m, j].astype(f32) + (decay_rate * decay_rate) * m_a[m, j].astype(f32)).astype(bf16)
        strip = xo_ref.at[m, x, :, 0:TOP, :]
        a4.append([send(strip, strip, at_x(dx)) for dx in x_peers])
        if m == 0:
            for copy in m4 + b3:
                copy.wait_recv()
        for i in range(NX):
            for j in range(NYH):
                xo_ref[m, i, j, TOP:SLAB, own_cols] = (
                    scale * all_b[m, i, j].astype(f32)
                    + (decay_rate * decay_rate) * m_b[m, i, j].astype(f32)).astype(bf16)
        strip = xo_ref.at[m, :, :, TOP:SLAB, own_cols]
        b4.append([send(strip, strip, at_z(dz)) for dz in z_peers])
    for m in range(MATS):
        for copy in a4[m] + b4[m]:
            copy.wait_recv()
    for copy in sent:
        copy.wait_send()


def comm(partials, momentum):
    z_n, yz_n, xy_n = NZ - 1, NYH * NZ - 1, NX * NYH - 1
    n_copies = 4 * (NX - 1) + 3 * z_n + 2 * yz_n + 2 * xy_n + 2 * z_n + xy_n + 1 + z_n + (NX * NC - 1) + (NYH * NYL - 1)
    return pl.pallas_call(
        comm_kernel,
        name="reduce_blend_gather",
        out_shape=jax.ShapeDtypeStruct((MATS, NX, NYH, SLAB, COLS), bf16),
        in_specs=[pl.BlockSpec(memory_space=pltpu.HBM), pl.BlockSpec(memory_space=pltpu.VMEM)],
        out_specs=pl.BlockSpec(memory_space=pltpu.VMEM),
        scratch_shapes=[
            pltpu.VMEM((MATS, NYH, TOP, COLS), bf16),
            pltpu.VMEM((MATS, NX, NYH, REST, WIDE), bf16),
            pltpu.VMEM((MATS, NX - 1, NYH, TOP, COLS), bf16),
            pltpu.VMEM((NZ - 1, MATS, NX, NYH, REST, WIDE), bf16),
            pltpu.VMEM((MATS, NYH, TOP, COLS), bf16),
            pltpu.VMEM((MATS, NX, NYH, REST, WIDE), bf16),
            pltpu.VMEM((NYH * NZ - 1, MATS, TOP, WIDE), bf16),
            pltpu.VMEM((NX * NYH - 1, MATS, REST, WIDE), bf16),
            pltpu.VMEM((MATS, NYH, TOP, COLS), bf16),
            pltpu.VMEM((MATS, NX, NYH, REST, WIDE), bf16),
            pltpu.VMEM((MATS, OWN_PAD, COLS), f32),
            pltpu.VMEM((NZ, MATS, OWN_PAD, WIDE), f32),
            pltpu.VMEM((MATS, NYH, TOP, WIDE), bf16),
            pltpu.VMEM((MATS, NYH, TOP, COLS), bf16),
            pltpu.VMEM((MATS, NX, NYH, REST, WIDE), bf16),
            pltpu.VMEM((3, 8, 8, WIDE), f32),
            pltpu.SemaphoreType.DMA((2,)),
            pltpu.SemaphoreType.DMA((n_copies,)),
            pltpu.SemaphoreType.DMA((n_copies,)),
        ],
        compiler_params=pltpu.CompilerParams(
            collective_id=0, has_side_effects=True, vmem_limit_bytes=32 << 20),
        cost_estimate=pl.CostEstimate(flops=10_000_000, bytes_accessed=8_000_000, transcendentals=0),
    )(partials, momentum)


def newton_kernel(x_ref, m_ref, u_ref, mo_ref, cur):
    x, yh, z, _, _ = place()
    final_scale = 0.2 * math.sqrt(max(ROWS, COLS))

    row = lax.broadcasted_iota(jnp.int32, (OWN_PAD, SLAB), 0)
    col = lax.broadcasted_iota(jnp.int32, (OWN_PAD, SLAB), 1)
    pick = ((col == z * OWN + row) & (row < OWN)).astype(f32).astype(bf16)
    for m in range(MATS):
        mine = jnp.dot(pick, x_ref[m, x, yh], preferred_element_type=f32)[0:OWN]
        old = m_ref[:, m, :]
        grad = (mine - (decay_rate * decay_rate) * old) * (1.0 / (1.0 + decay_rate))
        mo_ref[:, m, :] = decay_rate * old + grad

    for m in range(MATS):
        full = x_ref[m].reshape(ROWS, COLS).astype(f32)
        norm = jnp.sqrt(jnp.sum(jnp.sum(full * full, axis=1, keepdims=True), axis=0, keepdims=True))
        cur[m] = (full * (1.0 / (norm + 1e-07))).astype(bf16)

    def poly(m):
        here = cur[m]
        gram = lax.dot_general(here, here, (((1,), (1,)), ((), ())), preferred_element_type=f32).astype(bf16)
        square = jnp.dot(gram, gram, preferred_element_type=f32)
        return (coef_b * gram.astype(f32) + coef_c * square).astype(bf16)

    def step(_, carry):
        polys = [poly(m) for m in range(MATS)]
        for m in range(MATS):
            here = cur[m]
            cur[m] = (coef_a * here.astype(f32) + jnp.dot(polys[m], here, preferred_element_type=f32)).astype(bf16)
        return carry

    lax.fori_loop(0, ITERS - 1, step, 0)
    polys = [poly(m) for m in range(MATS)]
    for m in range(MATS):
        here = cur[m]
        last = coef_a * here.astype(f32) + jnp.dot(polys[m], here, preferred_element_type=f32)
        u_ref[m] = (last * final_scale).astype(bf16)


def newton(blended, momentum):
    vmem = pl.BlockSpec(memory_space=pltpu.VMEM)
    return pl.pallas_call(
        newton_kernel,
        name="newton_schulz",
        out_shape=(jax.ShapeDtypeStruct((MATS, ROWS, COLS), bf16), jax.ShapeDtypeStruct((OWN, MATS, COLS), f32)),
        in_specs=[vmem, vmem],
        out_specs=(vmem, vmem),
        scratch_shapes=[pltpu.VMEM((MATS, ROWS, COLS), bf16)],
        compiler_params=pltpu.CompilerParams(vmem_limit_bytes=40 << 20),
        cost_estimate=pl.CostEstimate(flops=7_200_000_000, bytes_accessed=3_200_000, transcendentals=0),
    )(blended, momentum)


def shards(partials, momentum):
    parts = partials.reshape(MATS, NX, NYH, SLAB, COLS)
    old = jnp.transpose(momentum[0], (1, 0, 2))
    blended = comm(parts, old)
    update, momentum_out = newton(blended, old)
    return update[None], jnp.transpose(momentum_out, (1, 0, 2))[None]


def solution(mesh):
    in_specs = (P("group", "dp", None, None, None), P("group", None, "dp", None))
    out_specs = (P("group", None, None, None), P("group", None, "dp", None))
    return jax.shard_map(shards, mesh=mesh, in_specs=in_specs, out_specs=out_specs, check_vma=False)
```

```python
import functools
import math

import jax
import jax.numpy as jnp
from jax import lax
from jax.experimental import pallas as pl
from jax.experimental.pallas import tpu as pltpu
from jax.sharding import PartitionSpec as P

MESH = pl.DeviceIdType.MESH

MATS = 2
ROWS = 384
COLS = 1024
ITERS = 5
EARLY = 4
GROUPS = 8

NX, NYH, NZ, NYL, NC = 4, 2, 8, 4, 2
SLAB = ROWS // (NX * NYH)
WIDE = COLS // NZ
TOP = SLAB * 2 // 3
REST = SLAB - TOP
OWN = SLAB // NZ
OWN_PAD = -(-OWN // 8) * 8

decay_rate = 0.95
coef_a = 3.4445
coef_b = -4.775
coef_c = 2.0315

bf16, f32 = jnp.bfloat16, jnp.float32


def place():
    d = lax.axis_index("dp")
    g = lax.axis_index("group")
    return d // (NYH * NZ), (d // NZ) % NYH, d % NZ, g // NC, g % NC


def dp_index(x, yh, z):
    return x * (NYH * NZ) + yh * NZ + z


def normalized(block):
    full = block.astype(f32)
    norm = jnp.sqrt(jnp.sum(jnp.sum(full * full, axis=1, keepdims=True), axis=0, keepdims=True))
    return (full * (1.0 / (norm + 1e-07))).astype(bf16)


def poly_of(here):
    gram = lax.dot_general(here, here, (((1,), (1,)), ((), ())), preferred_element_type=f32).astype(bf16)
    square = jnp.dot(gram, gram, preferred_element_type=f32)
    return (coef_b * gram.astype(f32) + coef_c * square).astype(bf16)


def stepped(here):
    return coef_a * here.astype(f32) + jnp.dot(poly_of(here), here, preferred_element_type=f32)


def comm_kernel(p_ref, m_ref, x1_ref, y0_ref, mo_ref, x0_ref, own_a, own_b, got_a, got_b, sum_a, sum_b, got_a2, got_b2,
                all_a, all_b, m_out, m_got, m_pair, m_a, m_b, q_got, lsem, ssem, rsem):
    x, yh, z, yl, core = place()
    xs = (x0_ref, x1_ref)
    counter = [0]

    def wrap(v, n):
        return lax.rem(v, n)

    sent = []

    def send(src, dst, device):
        i = counter[0]
        counter[0] += 1
        copy = pltpu.make_async_remote_copy(
            src_ref=src, dst_ref=dst, send_sem=ssem.at[i], recv_sem=rsem.at[i],
            device_id=device, device_id_type=MESH)
        copy.start()
        sent.append(copy)
        return copy

    x_peers = list(range(1, NX))
    z_peers = sorted(range(1, NZ), key=lambda d: -min(d, NZ - d))
    y_peers = list(range(1, NYH * NYL))
    yz_peers = [(dy, dz) for dy in range(NYH) for dz in range(NZ) if (dy, dz) != (0, 0)][::-1]
    xy_peers = [(dx, dy) for dx in range(NX) for dy in range(NYH) if (dx, dy) != (0, 0)][::-1]
    xc_peers = [(dx, dc) for dx in range(NX) for dc in range(NC) if (dx, dc) != (0, 0)]

    def at_z(dz):
        return {"dp": dp_index(x, yh, wrap(z + dz, NZ))}

    def at_x(dx):
        return {"dp": dp_index(wrap(x + dx, NX), yh, z)}

    def at_yz(t):
        return {"dp": dp_index(x, wrap(yh + t[0], NYH), wrap(z + t[1], NZ))}

    def at_xy(t):
        return {"dp": dp_index(wrap(x + t[0], NX), wrap(yh + t[1], NYH), z)}

    def at_xc(t):
        return {"group": yl * NC + wrap(core + t[1], NC), "dp": dp_index(wrap(x + t[0], NX), yh, z)}

    def at_y(dy):
        y = wrap(yh * NYL + yl + dy, NYH * NYL)
        return {"group": lax.rem(y, NYL) * NC + core, "dp": dp_index(x, y // NYL, z)}

    def cols_of(zz):
        return pl.ds(pl.multiple_of(zz * WIDE, WIDE), WIDE)

    own_cols = cols_of(z)

    local_a = pltpu.make_async_copy(p_ref.at[:, x, :, 0:TOP, :], own_a, lsem.at[0])
    local_b = pltpu.make_async_copy(p_ref.at[:, :, :, TOP:SLAB, own_cols], own_b, lsem.at[1])
    local_a.start()
    local_b.start()

    targets = [at_z(dz) for dz in z_peers] + [at_y(dy) for dy in y_peers] + [at_x(dx) for dx in x_peers]
    targets.append(at_xc((0, 1)))
    barrier = pltpu.get_barrier_semaphore()
    for device in targets:
        pl.semaphore_signal(barrier, inc=1, device_id=device, device_id_type=MESH)
    m_out[...] = jnp.zeros_like(m_out)
    for m in range(MATS):
        m_out[m, 0:OWN, :] = m_ref[:, m, :]
    m_got[z] = m_out[:, :, own_cols]
    pl.semaphore_wait(barrier, len(targets))

    m1 = [send(m_out.at[:, :, cols_of(wrap(z + dz, NZ))], m_got.at[z], at_z(dz)) for dz in z_peers]
    a1 = [[], []]
    b1 = []
    b_order = list(z_peers)

    def send_b():
        dz = b_order.pop(0)
        b1.append(send(p_ref.at[:, :, :, TOP:SLAB, cols_of(wrap(z + dz, NZ))], got_b.at[dz - 1], at_z(dz)))

    for m in range(MATS):
        for dx in x_peers:
            a1[m].append(send(p_ref.at[m, wrap(x + dx, NX), :, 0:TOP, :], got_a.at[m, dx - 1], at_x(dx)))
            if b_order:
                send_b()
    while b_order:
        send_b()

    row = lax.broadcasted_iota(jnp.int32, (SLAB, NZ * OWN_PAD), 0)
    slot = lax.broadcasted_iota(jnp.int32, (SLAB, NZ * OWN_PAD), 1)
    pick = ((slot // OWN_PAD) * OWN + slot % OWN_PAD == row) & (slot % OWN_PAD < OWN)
    pick = pick.astype(f32).astype(bf16)
    for copy in m1:
        copy.wait_recv()
    for m in range(MATS):
        block = jnp.dot(pick, m_got[:, m].reshape(NZ * OWN_PAD, WIDE).astype(bf16),
                        preferred_element_type=f32).astype(bf16)
        m_pair[m, yh] = block[0:TOP]
        m_b[m, x, yh] = block[TOP:SLAB]
    m2 = send(m_pair.at[:, yh], m_pair.at[:, yh], at_yz((1, 0)))

    local_a.wait()
    local_b.wait()
    a2 = []
    for m in range(MATS):
        for copy in a1[m]:
            copy.wait_recv()
        total = own_a[m].astype(f32)
        for j in range(NX - 1):
            total = total + got_a[m, j].astype(f32)
        sum_a[m] = total.astype(bf16)
        a2 += [send(sum_a.at[m, wrap(yh + t[0], NYH), :, cols_of(wrap(z + t[1], NZ))], got_a2.at[j, m], at_yz(t))
               for j, t in enumerate(yz_peers)]
    for copy in b1:
        copy.wait_recv()
    total = own_b[...].astype(f32)
    for j in range(NZ - 1):
        total = total + got_b[j].astype(f32)
    sum_b[...] = total.astype(bf16)
    b2 = [send(sum_b.at[:, wrap(x + t[0], NX), wrap(yh + t[1], NYH)], got_b2.at[j], at_xy(t))
          for j, t in enumerate(xy_peers)]

    m4 = [send(m_b.at[:, x, yh], m_b.at[:, x, yh], at_xy(t)) for t in xy_peers]
    m2.wait_recv()
    m_a[:, :, :, own_cols] = m_pair[...]
    m3 = [send(m_pair, m_a.at[:, :, :, own_cols], at_z(dz)) for dz in z_peers]

    for copy in a2:
        copy.wait_recv()
    top = sum_a[:, yh, :, own_cols].astype(f32)
    for j in range(len(yz_peers)):
        top = top + got_a2[j].astype(f32)
    for copy in b2:
        copy.wait_recv()
    rest = sum_b[:, x, yh].astype(f32)
    for j in range(len(xy_peers)):
        rest = rest + got_b2[j].astype(f32)

    square = jnp.zeros((8, WIDE), f32)
    for m in range(MATS):
        for part in (top[m], rest[m]):
            for r in range(0, part.shape[0], 8):
                square = square + part[r:r + 8] * part[r:r + 8]

    def spread(stage, mine, peers, at):
        q_got[stage, mine] = square
        here = q_got.at[stage, mine]
        return [send(here, here, at(t)) for t in peers]

    def gather(stage, copies):
        for copy in copies:
            copy.wait_recv()
        total = q_got[stage, 0]
        for j in range(1, len(copies) + 1):
            total = total + q_got[stage, j]
        return total

    q = spread(0, z, z_peers, at_z)
    all_a[:, yh, :, own_cols] = top.astype(bf16)
    all_b[:, x, yh] = rest.astype(bf16)
    here = all_a.at[:, yh, :, own_cols]
    a3 = [send(here, here, at_yz(t)) for t in yz_peers]
    here = all_b.at[:, x, yh]
    b3 = [send(here, here, at_xy(t)) for t in xy_peers]
    square = gather(0, q)
    q = spread(1, x * NC + core, xc_peers, at_xc)
    square = gather(1, q)
    q = spread(2, yh * NYL + yl, y_peers, at_y)
    square = gather(2, q)
    square_sum = jnp.sum(jnp.sum(square, axis=1, keepdims=True), axis=0, keepdims=True)
    entries = GROUPS * MATS * ROWS * COLS
    clip = jnp.minimum(1.0, math.sqrt(entries) / jnp.sqrt(square_sum + 1e-06))
    scale = (1.0 + decay_rate) * clip

    for copy in m3 + a3:
        copy.wait_recv()
    a4 = []
    b4 = []
    for m in range(MATS):
        for j in range(NYH):
            xs[m][x, j, 0:TOP, :] = (
                scale * all_a[m, j].astype(f32) + (decay_rate * decay_rate) * m_a[m, j].astype(f32)).astype(bf16)
        strip = xs[m].at[x, :, 0:TOP, :]
        a4.append([send(strip, strip, at_x(dx)) for dx in x_peers])
        if m == 0:
            for copy in m4 + b3:
                copy.wait_recv()
        for i in range(NX):
            for j in range(NYH):
                xs[m][i, j, TOP:SLAB, own_cols] = (
                    scale * all_b[m, i, j].astype(f32)
                    + (decay_rate * decay_rate) * m_b[m, i, j].astype(f32)).astype(bf16)
        strip = xs[m].at[:, :, TOP:SLAB, own_cols]
        b4.append([send(strip, strip, at_z(dz)) for dz in z_peers])

    for copy in a4[0] + b4[0]:
        copy.wait_recv()
    y0_ref[...] = normalized(x0_ref[...].reshape(ROWS, COLS))
    for _ in range(EARLY):
        y0_ref[...] = stepped(y0_ref[...]).astype(bf16)

    for copy in a4[1] + b4[1]:
        copy.wait_recv()

    row = lax.broadcasted_iota(jnp.int32, (OWN_PAD, SLAB), 0)
    col = lax.broadcasted_iota(jnp.int32, (OWN_PAD, SLAB), 1)
    pick = ((col == z * OWN + row) & (row < OWN)).astype(f32).astype(bf16)
    for m in range(MATS):
        mine = jnp.dot(pick, xs[m][x, yh], preferred_element_type=f32)[0:OWN]
        old = m_ref[:, m, :]
        grad = (mine - (decay_rate * decay_rate) * old) * (1.0 / (1.0 + decay_rate))
        mo_ref[:, m, :] = decay_rate * old + grad
    for copy in sent:
        copy.wait_send()


def comm(partials, momentum):
    z_n, yz_n, xy_n = NZ - 1, NYH * NZ - 1, NX * NYH - 1
    n_copies = 4 * (NX - 1) + 3 * z_n + 3 * yz_n + 2 * xy_n + 2 * z_n + xy_n + 1 + z_n + (NX * NC - 1) + (NYH * NYL - 1)
    return pl.pallas_call(
        comm_kernel,
        name="reduce_blend_gather",
        out_shape=(jax.ShapeDtypeStruct((NX, NYH, SLAB, COLS), bf16), jax.ShapeDtypeStruct((ROWS, COLS), bf16),
                   jax.ShapeDtypeStruct((OWN, MATS, COLS), f32)),
        in_specs=[pl.BlockSpec(memory_space=pltpu.HBM), pl.BlockSpec(memory_space=pltpu.VMEM)],
        out_specs=(pl.BlockSpec(memory_space=pltpu.VMEM),) * 3,
        scratch_shapes=[
            pltpu.VMEM((NX, NYH, SLAB, COLS), bf16),
            pltpu.VMEM((MATS, NYH, TOP, COLS), bf16),
            pltpu.VMEM((MATS, NX, NYH, REST, WIDE), bf16),
            pltpu.VMEM((MATS, NX - 1, NYH, TOP, COLS), bf16),
            pltpu.VMEM((NZ - 1, MATS, NX, NYH, REST, WIDE), bf16),
            pltpu.VMEM((MATS, NYH, TOP, COLS), bf16),
            pltpu.VMEM((MATS, NX, NYH, REST, WIDE), bf16),
            pltpu.VMEM((NYH * NZ - 1, MATS, TOP, WIDE), bf16),
            pltpu.VMEM((NX * NYH - 1, MATS, REST, WIDE), bf16),
            pltpu.VMEM((MATS, NYH, TOP, COLS), bf16),
            pltpu.VMEM((MATS, NX, NYH, REST, WIDE), bf16),
            pltpu.VMEM((MATS, OWN_PAD, COLS), f32),
            pltpu.VMEM((NZ, MATS, OWN_PAD, WIDE), f32),
            pltpu.VMEM((MATS, NYH, TOP, WIDE), bf16),
            pltpu.VMEM((MATS, NYH, TOP, COLS), bf16),
            pltpu.VMEM((MATS, NX, NYH, REST, WIDE), bf16),
            pltpu.VMEM((3, 8, 8, WIDE), f32),
            pltpu.SemaphoreType.DMA((2,)),
            pltpu.SemaphoreType.DMA((n_copies,)),
            pltpu.SemaphoreType.DMA((n_copies,)),
        ],
        compiler_params=pltpu.CompilerParams(
            collective_id=0, has_side_effects=True, vmem_limit_bytes=32 << 20),
        cost_estimate=pl.CostEstimate(flops=2_900_000_000, bytes_accessed=8_000_000, transcendentals=0),
    )(partials, momentum)


def newton_kernel(x1_ref, y0_ref, mi_ref, u_ref, mo_ref, cur, done, sem):
    final_scale = 0.2 * math.sqrt(max(ROWS, COLS))
    mo_ref[...] = mi_ref[...]
    copies = []

    def finish(m, value):
        done[m] = (value * final_scale).astype(bf16)
        copies.append(pltpu.make_async_copy(done.at[m], u_ref.at[m], sem.at[m]))
        copies[-1].start()

    cur[0] = y0_ref[...]
    cur[1] = normalized(x1_ref[...].reshape(ROWS, COLS))
    left = [ITERS - EARLY, ITERS]
    for _ in range(ITERS):
        work = [m for m in range(MATS) if left[m] > 0]
        polys = {m: poly_of(cur[m]) for m in work}
        for m in work:
            here = cur[m]
            value = coef_a * here.astype(f32) + jnp.dot(polys[m], here, preferred_element_type=f32)
            left[m] -= 1
            if left[m] > 0:
                cur[m] = value.astype(bf16)
            else:
                finish(m, value)
    for copy in copies:
        copy.wait()


def newton(x1, y0, momentum_out):
    vmem = pl.BlockSpec(memory_space=pltpu.VMEM)
    return pl.pallas_call(
        newton_kernel,
        name="newton_schulz",
        out_shape=(jax.ShapeDtypeStruct((MATS, ROWS, COLS), bf16), jax.ShapeDtypeStruct((OWN, MATS, COLS), f32)),
        in_specs=[vmem, vmem, vmem],
        out_specs=(pl.BlockSpec(memory_space=pltpu.HBM), vmem),
        scratch_shapes=[pltpu.VMEM((MATS, ROWS, COLS), bf16), pltpu.VMEM((MATS, ROWS, COLS), bf16),
                        pltpu.SemaphoreType.DMA((MATS,))],
        compiler_params=pltpu.CompilerParams(vmem_limit_bytes=40 << 20),
        cost_estimate=pl.CostEstimate(flops=4_300_000_000, bytes_accessed=3_200_000, transcendentals=0),
    )(x1, y0, momentum_out)


def shards(partials, momentum):
    parts = partials.reshape(MATS, NX, NYH, SLAB, COLS)
    old = jnp.transpose(momentum[0], (1, 0, 2))
    update, momentum_out = newton(*comm(parts, old))
    return update[None], jnp.transpose(momentum_out, (1, 0, 2))[None]


def solution(mesh):
    in_specs = (P("group", "dp", None, None, None), P("group", None, "dp", None))
    out_specs = (P("group", None, None, None), P("group", None, "dp", None))
    return jax.shard_map(shards, mesh=mesh, in_specs=in_specs, out_specs=out_specs, check_vma=False)
```

```python
import functools
import math

import jax
import jax.numpy as jnp
from jax import lax
from jax.experimental import pallas as pl
from jax.experimental.pallas import tpu as pltpu
from jax.sharding import PartitionSpec as P

MESH = pl.DeviceIdType.MESH

MATS = 2
ROWS = 384
COLS = 1024
ITERS = 5
GROUPS = 8

NX, NYH, NZ, NYL, NC = 4, 2, 8, 4, 2
SLAB = ROWS // (NX * NYH)
WIDE = COLS // NZ
TOP = SLAB * 2 // 3
REST = SLAB - TOP
OWN = SLAB // NZ
OWN_PAD = -(-OWN // 8) * 8

decay_rate = 0.95
coef_a = 3.4445
coef_b = -4.775
coef_c = 2.0315
FINAL_SCALE = 0.2 * math.sqrt(max(ROWS, COLS))

bf16, f32 = jnp.bfloat16, jnp.float32


def place():
    d = lax.axis_index("dp")
    g = lax.axis_index("group")
    return d // (NYH * NZ), (d // NZ) % NYH, d % NZ, g // NC, g % NC


def dp_index(x, yh, z):
    return x * (NYH * NZ) + yh * NZ + z


def normalized(block):
    full = block.astype(f32)
    norm = jnp.sqrt(jnp.sum(jnp.sum(full * full, axis=1, keepdims=True), axis=0, keepdims=True))
    return (full * (1.0 / (norm + 1e-07))).astype(bf16)


def poly_of(here):
    gram = lax.dot_general(here, here, (((1,), (1,)), ((), ())), preferred_element_type=f32).astype(bf16)
    square = jnp.dot(gram, gram, preferred_element_type=f32)
    return (coef_b * gram.astype(f32) + coef_c * square).astype(bf16)


def stepped(here):
    return coef_a * here.astype(f32) + jnp.dot(poly_of(here), here, preferred_element_type=f32)


def comm_kernel(p_ref, m_ref, x1_ref, y0_ref, mo_ref, x0_ref, own_a, own_b, got_a, got_b, sum_a, sum_b, got_a2, got_b2,
                all_a, all_b, m_out, m_got, m_pair, m_a, m_b, q_got, lsem, ssem, rsem):
    x, yh, z, yl, core = place()
    xs = (x0_ref, x1_ref)
    counter = [0]

    def wrap(v, n):
        return lax.rem(v, n)

    sent = []

    def send(src, dst, device):
        i = counter[0]
        counter[0] += 1
        copy = pltpu.make_async_remote_copy(
            src_ref=src, dst_ref=dst, send_sem=ssem.at[i], recv_sem=rsem.at[i],
            device_id=device, device_id_type=MESH)
        copy.start()
        sent.append(copy)
        return copy

    x_peers = list(range(1, NX))
    z_peers = sorted(range(1, NZ), key=lambda d: -min(d, NZ - d))
    y_peers = list(range(1, NYH * NYL))
    yz_peers = [(dy, dz) for dy in range(NYH) for dz in range(NZ) if (dy, dz) != (0, 0)][::-1]
    xy_peers = [(dx, dy) for dx in range(NX) for dy in range(NYH) if (dx, dy) != (0, 0)][::-1]
    xc_peers = [(dx, dc) for dx in range(NX) for dc in range(NC) if (dx, dc) != (0, 0)]

    def at_z(dz):
        return {"dp": dp_index(x, yh, wrap(z + dz, NZ))}

    def at_x(dx):
        return {"dp": dp_index(wrap(x + dx, NX), yh, z)}

    def at_yz(t):
        return {"dp": dp_index(x, wrap(yh + t[0], NYH), wrap(z + t[1], NZ))}

    def at_xy(t):
        return {"dp": dp_index(wrap(x + t[0], NX), wrap(yh + t[1], NYH), z)}

    def at_xc(t):
        return {"group": yl * NC + wrap(core + t[1], NC), "dp": dp_index(wrap(x + t[0], NX), yh, z)}

    def at_y(dy):
        y = wrap(yh * NYL + yl + dy, NYH * NYL)
        return {"group": lax.rem(y, NYL) * NC + core, "dp": dp_index(x, y // NYL, z)}

    def cols_of(zz):
        return pl.ds(pl.multiple_of(zz * WIDE, WIDE), WIDE)

    own_cols = cols_of(z)

    local_a = pltpu.make_async_copy(p_ref.at[:, x, :, 0:TOP, :], own_a, lsem.at[0])
    local_b = pltpu.make_async_copy(p_ref.at[:, :, :, TOP:SLAB, own_cols], own_b, lsem.at[1])
    local_a.start()
    local_b.start()

    targets = [at_z(dz) for dz in z_peers] + [at_y(dy) for dy in y_peers] + [at_x(dx) for dx in x_peers]
    targets.append(at_xc((0, 1)))
    barrier = pltpu.get_barrier_semaphore()
    for device in targets:
        pl.semaphore_signal(barrier, inc=1, device_id=device, device_id_type=MESH)
    m_out[...] = jnp.zeros_like(m_out)
    for m in range(MATS):
        m_out[m, 0:OWN, :] = m_ref[:, m, :]
    m_got[z] = m_out[:, :, own_cols]
    pl.semaphore_wait(barrier, len(targets))

    m1 = [send(m_out.at[:, :, cols_of(wrap(z + dz, NZ))], m_got.at[z], at_z(dz)) for dz in z_peers]
    a1 = [[], []]
    b1 = []
    b_order = list(z_peers)

    def send_b():
        dz = b_order.pop(0)
        b1.append(send(p_ref.at[:, :, :, TOP:SLAB, cols_of(wrap(z + dz, NZ))], got_b.at[dz - 1], at_z(dz)))

    for m in range(MATS):
        for dx in x_peers:
            a1[m].append(send(p_ref.at[m, wrap(x + dx, NX), :, 0:TOP, :], got_a.at[m, dx - 1], at_x(dx)))
            if b_order:
                send_b()
    while b_order:
        send_b()

    row = lax.broadcasted_iota(jnp.int32, (SLAB, NZ * OWN_PAD), 0)
    slot = lax.broadcasted_iota(jnp.int32, (SLAB, NZ * OWN_PAD), 1)
    pick = ((slot // OWN_PAD) * OWN + slot % OWN_PAD == row) & (slot % OWN_PAD < OWN)
    pick = pick.astype(f32).astype(bf16)
    for copy in m1:
        copy.wait_recv()
    for m in range(MATS):
        block = jnp.dot(pick, m_got[:, m].reshape(NZ * OWN_PAD, WIDE).astype(bf16),
                        preferred_element_type=f32).astype(bf16)
        m_pair[m, yh] = block[0:TOP]
        m_b[m, x, yh] = block[TOP:SLAB]
    m2 = send(m_pair.at[:, yh], m_pair.at[:, yh], at_yz((1, 0)))

    local_a.wait()
    local_b.wait()
    a2 = []
    for m in range(MATS):
        for copy in a1[m]:
            copy.wait_recv()
        total = own_a[m].astype(f32)
        for j in range(NX - 1):
            total = total + got_a[m, j].astype(f32)
        sum_a[m] = total.astype(bf16)
        a2 += [send(sum_a.at[m, wrap(yh + t[0], NYH), :, cols_of(wrap(z + t[1], NZ))], got_a2.at[j, m], at_yz(t))
               for j, t in enumerate(yz_peers)]
        if m == 0:
            m4 = [send(m_b.at[:, x, yh], m_b.at[:, x, yh], at_xy(t)) for t in xy_peers]
            m2.wait_recv()
            m_a[:, :, :, own_cols] = m_pair[...]
            m3 = [send(m_pair, m_a.at[:, :, :, own_cols], at_z(dz)) for dz in z_peers]
    for copy in b1:
        copy.wait_recv()
    total = own_b[...].astype(f32)
    for j in range(NZ - 1):
        total = total + got_b[j].astype(f32)
    sum_b[...] = total.astype(bf16)
    b2 = [send(sum_b.at[:, wrap(x + t[0], NX), wrap(yh + t[1], NYH)], got_b2.at[j], at_xy(t))
          for j, t in enumerate(xy_peers)]

    for copy in a2:
        copy.wait_recv()
    top = sum_a[:, yh, :, own_cols].astype(f32)
    for j in range(len(yz_peers)):
        top = top + got_a2[j].astype(f32)
    for copy in b2:
        copy.wait_recv()
    rest = sum_b[:, x, yh].astype(f32)
    for j in range(len(xy_peers)):
        rest = rest + got_b2[j].astype(f32)

    square = jnp.zeros((8, WIDE), f32)
    for m in range(MATS):
        for part in (top[m], rest[m]):
            for r in range(0, part.shape[0], 8):
                square = square + part[r:r + 8] * part[r:r + 8]

    def spread(stage, mine, peers, at):
        q_got[stage, mine] = square
        here = q_got.at[stage, mine]
        return [send(here, here, at(t)) for t in peers]

    def gather(stage, copies):
        for copy in copies:
            copy.wait_recv()
        total = q_got[stage, 0]
        for j in range(1, len(copies) + 1):
            total = total + q_got[stage, j]
        return total

    q = spread(0, yh * NYL + yl, y_peers, at_y)
    all_a[:, yh, :, own_cols] = top.astype(bf16)
    all_b[:, x, yh] = rest.astype(bf16)
    here = all_a.at[:, yh, :, own_cols]
    a3 = [send(here, here, at_yz(t)) for t in yz_peers]
    here = all_b.at[:, x, yh]
    b3 = [send(here, here, at_xy(t)) for t in xy_peers]
    square = gather(0, q)
    q = spread(1, z, z_peers, at_z)
    square = gather(1, q)
    q = spread(2, x * NC + core, xc_peers, at_xc)
    square = gather(2, q)
    square_sum = jnp.sum(jnp.sum(square, axis=1, keepdims=True), axis=0, keepdims=True)
    entries = GROUPS * MATS * ROWS * COLS
    clip = jnp.minimum(1.0, math.sqrt(entries) / jnp.sqrt(square_sum + 1e-06))
    scale = (1.0 + decay_rate) * clip

    for copy in m3 + a3:
        copy.wait_recv()
    a4 = []
    b4 = []
    for m in range(MATS):
        for j in range(NYH):
            xs[m][x, j, 0:TOP, :] = (
                scale * all_a[m, j].astype(f32) + (decay_rate * decay_rate) * m_a[m, j].astype(f32)).astype(bf16)
        strip = xs[m].at[x, :, 0:TOP, :]
        a4.append([send(strip, strip, at_x(dx)) for dx in x_peers])
        if m == 0:
            for copy in m4 + b3:
                copy.wait_recv()
        for i in range(NX):
            for j in range(NYH):
                xs[m][i, j, TOP:SLAB, own_cols] = (
                    scale * all_b[m, i, j].astype(f32)
                    + (decay_rate * decay_rate) * m_b[m, i, j].astype(f32)).astype(bf16)
        strip = xs[m].at[:, :, TOP:SLAB, own_cols]
        b4.append([send(strip, strip, at_z(dz)) for dz in z_peers])

    for copy in a4[0] + b4[0]:
        copy.wait_recv()
    y0_ref[...] = normalized(x0_ref[...].reshape(ROWS, COLS))
    for _ in range(ITERS - 1):
        y0_ref[...] = stepped(y0_ref[...]).astype(bf16)
    y0_ref[...] = (stepped(y0_ref[...]) * FINAL_SCALE).astype(bf16)

    for copy in a4[1] + b4[1]:
        copy.wait_recv()

    row = lax.broadcasted_iota(jnp.int32, (OWN_PAD, SLAB), 0)
    col = lax.broadcasted_iota(jnp.int32, (OWN_PAD, SLAB), 1)
    pick = ((col == z * OWN + row) & (row < OWN)).astype(f32).astype(bf16)
    for m in range(MATS):
        mine = jnp.dot(pick, xs[m][x, yh], preferred_element_type=f32)[0:OWN]
        old = m_ref[:, m, :]
        grad = (mine - (decay_rate * decay_rate) * old) * (1.0 / (1.0 + decay_rate))
        mo_ref[:, m, :] = decay_rate * old + grad
    for copy in sent:
        copy.wait_send()


def comm(partials, momentum):
    z_n, yz_n, xy_n = NZ - 1, NYH * NZ - 1, NX * NYH - 1
    n_copies = 4 * (NX - 1) + 3 * z_n + 3 * yz_n + 2 * xy_n + 2 * z_n + xy_n + 1 + z_n + (NX * NC - 1) + (NYH * NYL - 1)
    return pl.pallas_call(
        comm_kernel,
        name="reduce_blend_gather",
        out_shape=(jax.ShapeDtypeStruct((NX, NYH, SLAB, COLS), bf16), jax.ShapeDtypeStruct((ROWS, COLS), bf16),
                   jax.ShapeDtypeStruct((OWN, MATS, COLS), f32)),
        in_specs=[pl.BlockSpec(memory_space=pltpu.HBM), pl.BlockSpec(memory_space=pltpu.VMEM)],
        out_specs=(pl.BlockSpec(memory_space=pltpu.VMEM),) * 3,
        scratch_shapes=[
            pltpu.VMEM((NX, NYH, SLAB, COLS), bf16),
            pltpu.VMEM((MATS, NYH, TOP, COLS), bf16),
            pltpu.VMEM((MATS, NX, NYH, REST, WIDE), bf16),
            pltpu.VMEM((MATS, NX - 1, NYH, TOP, COLS), bf16),
            pltpu.VMEM((NZ - 1, MATS, NX, NYH, REST, WIDE), bf16),
            pltpu.VMEM((MATS, NYH, TOP, COLS), bf16),
            pltpu.VMEM((MATS, NX, NYH, REST, WIDE), bf16),
            pltpu.VMEM((NYH * NZ - 1, MATS, TOP, WIDE), bf16),
            pltpu.VMEM((NX * NYH - 1, MATS, REST, WIDE), bf16),
            pltpu.VMEM((MATS, NYH, TOP, COLS), bf16),
            pltpu.VMEM((MATS, NX, NYH, REST, WIDE), bf16),
            pltpu.VMEM((MATS, OWN_PAD, COLS), f32),
            pltpu.VMEM((NZ, MATS, OWN_PAD, WIDE), f32),
            pltpu.VMEM((MATS, NYH, TOP, WIDE), bf16),
            pltpu.VMEM((MATS, NYH, TOP, COLS), bf16),
            pltpu.VMEM((MATS, NX, NYH, REST, WIDE), bf16),
            pltpu.VMEM((3, 8, 8, WIDE), f32),
            pltpu.SemaphoreType.DMA((2,)),
            pltpu.SemaphoreType.DMA((n_copies,)),
            pltpu.SemaphoreType.DMA((n_copies,)),
        ],
        compiler_params=pltpu.CompilerParams(
            collective_id=0, has_side_effects=True, vmem_limit_bytes=52 << 20),
        cost_estimate=pl.CostEstimate(flops=2_900_000_000, bytes_accessed=8_000_000, transcendentals=0),
    )(partials, momentum)


def newton_kernel(x1_ref, y0_ref, mi_ref, u_ref, mo_ref, cur, sem):
    first = pltpu.make_async_copy(y0_ref, u_ref.at[0], sem.at[0])
    first.start()
    mo_ref[...] = mi_ref[...]
    cur[...] = normalized(x1_ref[...].reshape(ROWS, COLS))
    for _ in range(ITERS - 1):
        cur[...] = stepped(cur[...]).astype(bf16)
    cur[...] = (stepped(cur[...]) * FINAL_SCALE).astype(bf16)
    second = pltpu.make_async_copy(cur, u_ref.at[1], sem.at[1])
    second.start()
    first.wait()
    second.wait()


def newton(x1, y0, momentum_out):
    vmem = pl.BlockSpec(memory_space=pltpu.VMEM)
    return pl.pallas_call(
        newton_kernel,
        name="newton_schulz",
        out_shape=(jax.ShapeDtypeStruct((MATS, ROWS, COLS), bf16), jax.ShapeDtypeStruct((OWN, MATS, COLS), f32)),
        in_specs=[vmem, vmem, vmem],
        out_specs=(pl.BlockSpec(memory_space=pltpu.HBM), vmem),
        scratch_shapes=[pltpu.VMEM((ROWS, COLS), bf16), pltpu.SemaphoreType.DMA((MATS,))],
        compiler_params=pltpu.CompilerParams(vmem_limit_bytes=40 << 20),
        cost_estimate=pl.CostEstimate(flops=4_300_000_000, bytes_accessed=3_200_000, transcendentals=0),
    )(x1, y0, momentum_out)


def shards(partials, momentum):
    parts = partials.reshape(MATS, NX, NYH, SLAB, COLS)
    old = jnp.transpose(momentum[0], (1, 0, 2))
    update, momentum_out = newton(*comm(parts, old))
    return update[None], jnp.transpose(momentum_out, (1, 0, 2))[None]


def solution(mesh):
    in_specs = (P("group", "dp", None, None, None), P("group", None, "dp", None))
    out_specs = (P("group", None, None, None), P("group", None, "dp", None))
    return jax.shard_map(shards, mesh=mesh, in_specs=in_specs, out_specs=out_specs, check_vma=False)
```

```python
import functools
import math

import jax
import jax.numpy as jnp
from jax import lax
from jax.experimental import pallas as pl
from jax.experimental.pallas import tpu as pltpu
from jax.sharding import PartitionSpec as P

MESH = pl.DeviceIdType.MESH

MATS = 2
ROWS = 384
COLS = 1024
ITERS = 5
PIECES = 2
GROUPS = 8

NX, NYH, NZ, NYL, NC = 4, 2, 8, 4, 2
SLAB = ROWS // (NX * NYH)
WIDE = COLS // NZ
TOP = SLAB * 2 // 3
REST = SLAB - TOP
OWN = SLAB // NZ
OWN_PAD = -(-OWN // 8) * 8

decay_rate = 0.95
coef_a = 3.4445
coef_b = -4.775
coef_c = 2.0315
FINAL_SCALE = 0.2 * math.sqrt(max(ROWS, COLS))

bf16, f32 = jnp.bfloat16, jnp.float32


def place():
    d = lax.axis_index("dp")
    g = lax.axis_index("group")
    return d // (NYH * NZ), (d // NZ) % NYH, d % NZ, g // NC, g % NC


def dp_index(x, yh, z):
    return x * (NYH * NZ) + yh * NZ + z


def normalized(block):
    full = block.astype(f32)
    norm = jnp.sqrt(jnp.sum(jnp.sum(full * full, axis=1, keepdims=True), axis=0, keepdims=True))
    return (full * (1.0 / (norm + 1e-07))).astype(bf16)


def poly_of(here):
    gram = lax.dot_general(here, here, (((1,), (1,)), ((), ())), preferred_element_type=f32).astype(bf16)
    square = jnp.dot(gram, gram, preferred_element_type=f32)
    return (coef_b * gram.astype(f32) + coef_c * square).astype(bf16)


def stepped(here):
    return coef_a * here.astype(f32) + jnp.dot(poly_of(here), here, preferred_element_type=f32)


def comm_kernel(p_ref, m_ref, x1_ref, y0_ref, mo_ref, own_a, own_b, got_a, got_b, sum_a, sum_b, got_a2, got_b2,
                s_all, m_all, m_out, m_got, q_got, lsem, ssem, rsem):
    x, yh, z, yl, core = place()
    counter = [0]

    def wrap(v, n):
        return lax.rem(v, n)

    sent = []

    def send(src, dst, device):
        i = counter[0]
        counter[0] += 1
        copy = pltpu.make_async_remote_copy(
            src_ref=src, dst_ref=dst, send_sem=ssem.at[i], recv_sem=rsem.at[i],
            device_id=device, device_id_type=MESH)
        copy.start()
        sent.append(copy)
        return copy

    x_peers = list(range(1, NX))
    z_peers = sorted(range(1, NZ), key=lambda d: -min(d, NZ - d))
    y_peers = list(range(1, NYH * NYL))
    yz_peers = [(dy, dz) for dy in range(NYH) for dz in range(NZ) if (dy, dz) != (0, 0)][::-1]
    xy_peers = [(dx, dy) for dx in range(NX) for dy in range(NYH) if (dx, dy) != (0, 0)][::-1]
    xc_peers = [(dx, dc) for dx in range(NX) for dc in range(NC) if (dx, dc) != (0, 0)]

    def at_z(dz):
        return {"dp": dp_index(x, yh, wrap(z + dz, NZ))}

    def at_x(dx):
        return {"dp": dp_index(wrap(x + dx, NX), yh, z)}

    def at_yz(t):
        return {"dp": dp_index(x, wrap(yh + t[0], NYH), wrap(z + t[1], NZ))}

    def at_xy(t):
        return {"dp": dp_index(wrap(x + t[0], NX), wrap(yh + t[1], NYH), z)}

    def at_xc(t):
        return {"group": yl * NC + wrap(core + t[1], NC), "dp": dp_index(wrap(x + t[0], NX), yh, z)}

    def at_y(dy):
        y = wrap(yh * NYL + yl + dy, NYH * NYL)
        return {"group": lax.rem(y, NYL) * NC + core, "dp": dp_index(x, y // NYL, z)}

    def cols_of(zz):
        return pl.ds(pl.multiple_of(zz * WIDE, WIDE), WIDE)

    own_cols = cols_of(z)

    local_a = pltpu.make_async_copy(p_ref.at[:, x, :, 0:TOP, :], own_a, lsem.at[0])
    local_b = pltpu.make_async_copy(p_ref.at[:, :, :, TOP:SLAB, own_cols], own_b, lsem.at[1])
    local_a.start()
    local_b.start()

    targets = [at_z(dz) for dz in z_peers] + [at_y(dy) for dy in y_peers] + [at_x(dx) for dx in x_peers]
    targets.append(at_xc((0, 1)))
    barrier = pltpu.get_barrier_semaphore()
    for device in targets:
        pl.semaphore_signal(barrier, inc=1, device_id=device, device_id_type=MESH)
    m_out[...] = jnp.zeros_like(m_out)
    for m in range(MATS):
        m_out[m, 0:OWN, :] = m_ref[:, m, :]
    m_got[z] = m_out[:, :, own_cols]
    pl.semaphore_wait(barrier, len(targets))

    m1 = [send(m_out.at[:, :, cols_of(wrap(z + dz, NZ))], m_got.at[z], at_z(dz)) for dz in z_peers]
    a1 = [[], []]
    b1 = []
    b_order = list(z_peers)

    def send_b():
        dz = b_order.pop(0)
        b1.append(send(p_ref.at[:, :, :, TOP:SLAB, cols_of(wrap(z + dz, NZ))], got_b.at[dz - 1], at_z(dz)))

    for m in range(MATS):
        for dx in x_peers:
            a1[m].append(send(p_ref.at[m, wrap(x + dx, NX), :, 0:TOP, :], got_a.at[m, dx - 1], at_x(dx)))
            if b_order:
                send_b()
    while b_order:
        send_b()

    row = lax.broadcasted_iota(jnp.int32, (SLAB, NZ * OWN_PAD), 0)
    slot = lax.broadcasted_iota(jnp.int32, (SLAB, NZ * OWN_PAD), 1)
    pick = ((slot // OWN_PAD) * OWN + slot % OWN_PAD == row) & (slot % OWN_PAD < OWN)
    pick = pick.astype(f32).astype(bf16)
    for copy in m1:
        copy.wait_recv()
    for m in range(MATS):
        block = jnp.dot(pick, m_got[:, m].reshape(NZ * OWN_PAD, WIDE).astype(bf16),
                        preferred_element_type=f32).astype(bf16)
        m_all[m, x, yh, :, own_cols] = block
    here = m_all.at[:, x, yh, :, own_cols]
    m2 = send(here, here, at_yz((1, 0)))

    def hop(t, before):
        for copy in before:
            copy.wait_recv()
        strip = m_all.at[:, x, :, :, cols_of(wrap(z + NZ - t + 1, NZ))]
        copies = [send(strip, strip, at_z(1))]
        if t < NZ // 2:
            strip = m_all.at[:, x, :, :, cols_of(wrap(z + t - 1, NZ))]
            copies.append(send(strip, strip, at_z(NZ - 1)))
        return copies


    local_a.wait()
    local_b.wait()
    a2 = []
    for m in range(MATS):
        for copy in a1[m]:
            copy.wait_recv()
        total = own_a[m].astype(f32)
        for j in range(NX - 1):
            total = total + got_a[m, j].astype(f32)
        sum_a[m] = total.astype(bf16)
        a2 += [send(sum_a.at[m, wrap(yh + t[0], NYH), :, cols_of(wrap(z + t[1], NZ))], got_a2.at[j, m], at_yz(t))
               for j, t in enumerate(yz_peers)]
        hops = hop(1, [m2]) if m == 0 else hop(2, hops)
    for copy in b1:
        copy.wait_recv()
    total = own_b[...].astype(f32)
    for j in range(NZ - 1):
        total = total + got_b[j].astype(f32)
    sum_b[...] = total.astype(bf16)
    b2 = [send(sum_b.at[:, wrap(x + t[0], NX), wrap(yh + t[1], NYH)], got_b2.at[j], at_xy(t))
          for j, t in enumerate(xy_peers)]

    for t in range(3, NZ // 2 + 1):
        hops = hop(t, hops)
    for copy in hops:
        copy.wait_recv()
    m3 = [[send(m_all.at[m, x], m_all.at[m, x], at_x(dx)) for dx in x_peers] for m in range(MATS)]

    for copy in a2:
        copy.wait_recv()
    top = sum_a[:, yh, :, own_cols].astype(f32)
    for j in range(len(yz_peers)):
        top = top + got_a2[j].astype(f32)
    for copy in b2:
        copy.wait_recv()
    rest = sum_b[:, x, yh].astype(f32)
    for j in range(len(xy_peers)):
        rest = rest + got_b2[j].astype(f32)

    square = jnp.zeros((8, WIDE), f32)
    for m in range(MATS):
        for part in (top[m], rest[m]):
            for r in range(0, part.shape[0], 8):
                square = square + part[r:r + 8] * part[r:r + 8]

    def spread(stage, mine, peers, at):
        q_got[stage, mine] = square
        here = q_got.at[stage, mine]
        return [send(here, here, at(t)) for t in peers]

    def gather(stage, copies):
        for copy in copies:
            copy.wait_recv()
        total = q_got[stage, 0]
        for j in range(1, len(copies) + 1):
            total = total + q_got[stage, j]
        return total

    q = spread(0, z, z_peers, at_z)
    a3 = []
    for m in range(MATS):
        s_all[m, x, yh, 0:TOP, own_cols] = top[m].astype(bf16)
        s_all[m, x, yh, TOP:SLAB, own_cols] = rest[m].astype(bf16)
        here = s_all.at[m, x, yh, :, own_cols]
        a3.append([send(here, here, at_yz(t)) for t in yz_peers])

    def onward(m):
        for copy in a3[m]:
            copy.wait_recv()
        strip = s_all.at[m, x]
        return [send(strip, strip, at_x(dx)) for dx in x_peers]

    square = gather(0, q)
    q = spread(1, x * NC + core, xc_peers, at_xc)
    a4 = [onward(0)]
    square = gather(1, q)
    q = spread(2, yh * NYL + yl, y_peers, at_y)
    a4.append(onward(1))
    square = gather(2, q)
    square_sum = jnp.sum(jnp.sum(square, axis=1, keepdims=True), axis=0, keepdims=True)
    entries = GROUPS * MATS * ROWS * COLS
    clip = jnp.minimum(1.0, math.sqrt(entries) / jnp.sqrt(square_sum + 1e-06))
    scale = (1.0 + decay_rate) * clip

    def blended(m):
        for copy in m3[m] + a4[m]:
            copy.wait_recv()
        total = s_all[m].reshape(ROWS, COLS).astype(f32)
        old = m_all[m].reshape(ROWS, COLS).astype(f32)
        return (scale * total + (decay_rate * decay_rate) * old).astype(bf16)

    row = lax.broadcasted_iota(jnp.int32, (OWN_PAD, SLAB), 0)
    col = lax.broadcasted_iota(jnp.int32, (OWN_PAD, SLAB), 1)
    pick = ((col == z * OWN + row) & (row < OWN)).astype(f32).astype(bf16)
    for m in range(MATS):
        mine = jnp.dot(pick, s_all[m, x, yh], preferred_element_type=f32)[0:OWN]
        mo_ref[:, m, :] = decay_rate * m_ref[:, m, :] + clip * mine

    y0_ref[...] = normalized(blended(0))
    for _ in range(ITERS - 2):
        y0_ref[...] = stepped(y0_ref[...]).astype(bf16)
    x1_ref[...] = normalized(blended(1))
    y0_ref[...] = stepped(y0_ref[...]).astype(bf16)
    y0_ref[...] = (stepped(y0_ref[...]) * FINAL_SCALE).astype(bf16)
    for copy in sent:
        copy.wait_send()


def comm(partials, momentum):
    z_n, yz_n, xy_n = NZ - 1, NYH * NZ - 1, NX * NYH - 1
    n_copies = 6 * (NX - 1) + 3 * z_n + 1 + 4 * yz_n + xy_n + z_n + (NX * NC - 1) + (NYH * NYL - 1)
    return pl.pallas_call(
        comm_kernel,
        name="reduce_blend_gather",
        out_shape=(jax.ShapeDtypeStruct((ROWS, COLS), bf16), jax.ShapeDtypeStruct((ROWS, COLS), bf16),
                   jax.ShapeDtypeStruct((OWN, MATS, COLS), f32)),
        in_specs=[pl.BlockSpec(memory_space=pltpu.HBM), pl.BlockSpec(memory_space=pltpu.VMEM)],
        out_specs=(pl.BlockSpec(memory_space=pltpu.VMEM),) * 3,
        scratch_shapes=[
            pltpu.VMEM((MATS, NYH, TOP, COLS), bf16),
            pltpu.VMEM((MATS, NX, NYH, REST, WIDE), bf16),
            pltpu.VMEM((MATS, NX - 1, NYH, TOP, COLS), bf16),
            pltpu.VMEM((NZ - 1, MATS, NX, NYH, REST, WIDE), bf16),
            pltpu.VMEM((MATS, NYH, TOP, COLS), bf16),
            pltpu.VMEM((MATS, NX, NYH, REST, WIDE), bf16),
            pltpu.VMEM((NYH * NZ - 1, MATS, TOP, WIDE), bf16),
            pltpu.VMEM((NX * NYH - 1, MATS, REST, WIDE), bf16),
            pltpu.VMEM((MATS, NX, NYH, SLAB, COLS), bf16),
            pltpu.VMEM((MATS, NX, NYH, SLAB, COLS), bf16),
            pltpu.VMEM((MATS, OWN_PAD, COLS), f32),
            pltpu.VMEM((NZ, MATS, OWN_PAD, WIDE), f32),
            pltpu.VMEM((3, 8, 8, WIDE), f32),
            pltpu.SemaphoreType.DMA((2,)),
            pltpu.SemaphoreType.DMA((n_copies,)),
            pltpu.SemaphoreType.DMA((n_copies,)),
        ],
        compiler_params=pltpu.CompilerParams(
            collective_id=0, has_side_effects=True, vmem_limit_bytes=52 << 20),
        cost_estimate=pl.CostEstimate(flops=2_900_000_000, bytes_accessed=8_000_000, transcendentals=0),
    )(partials, momentum)


def newton_kernel(x1_ref, y0_ref, mi_ref, u_ref, mo_ref, cur, sem):
    copies = [pltpu.make_async_copy(y0_ref, u_ref.at[0], sem.at[0])]
    copies[0].start()
    mo_ref[...] = mi_ref[...]
    here = x1_ref[...]
    for _ in range(ITERS - 1):
        here = stepped(here).astype(bf16)
    poly = poly_of(here)
    for i in range(PIECES):
        cols = slice(i * COLS // PIECES, (i + 1) * COLS // PIECES)
        part = here[:, cols]
        last = coef_a * part.astype(f32) + jnp.dot(poly, part, preferred_element_type=f32)
        cur[:, cols] = (last * FINAL_SCALE).astype(bf16)
        copies.append(pltpu.make_async_copy(cur.at[:, cols], u_ref.at[1, :, cols], sem.at[1 + i]))
        copies[-1].start()
    for copy in copies:
        copy.wait()


def newton(x1, y0, momentum_out):
    vmem = pl.BlockSpec(memory_space=pltpu.VMEM)
    return pl.pallas_call(
        newton_kernel,
        name="newton_schulz",
        out_shape=(jax.ShapeDtypeStruct((MATS, ROWS, COLS), bf16), jax.ShapeDtypeStruct((OWN, MATS, COLS), f32)),
        in_specs=[vmem, vmem, vmem],
        out_specs=(pl.BlockSpec(memory_space=pltpu.HBM), vmem),
        scratch_shapes=[pltpu.VMEM((ROWS, COLS), bf16), pltpu.SemaphoreType.DMA((1 + PIECES,))],
        compiler_params=pltpu.CompilerParams(vmem_limit_bytes=40 << 20),
        cost_estimate=pl.CostEstimate(flops=4_300_000_000, bytes_accessed=3_200_000, transcendentals=0),
    )(x1, y0, momentum_out)


def shards(partials, momentum):
    parts = partials.reshape(MATS, NX, NYH, SLAB, COLS)
    old = jnp.transpose(momentum[0], (1, 0, 2))
    update, momentum_out = newton(*comm(parts, old))
    return update[None], jnp.transpose(momentum_out, (1, 0, 2))[None]


def solution(mesh):
    in_specs = (P("group", "dp", None, None, None), P("group", None, "dp", None))
    out_specs = (P("group", None, None, None), P("group", None, "dp", None))
    return jax.shard_map(shards, mesh=mesh, in_specs=in_specs, out_specs=out_specs, check_vma=False)
```

```python
import functools
import math

import jax
import jax.numpy as jnp
from jax import lax
from jax.experimental import pallas as pl
from jax.experimental.pallas import tpu as pltpu
from jax.sharding import PartitionSpec as P

MESH = pl.DeviceIdType.MESH

MATS = 2
ROWS = 384
COLS = 1024
ITERS = 5
PIECES = 2
GROUPS = 8

NX, NYH, NZ, NYL, NC = 4, 2, 8, 4, 2
SLAB = ROWS // (NX * NYH)
WIDE = COLS // NZ
TOP = SLAB * 2 // 3
REST = SLAB - TOP
OWN = SLAB // NZ
OWN_PAD = -(-OWN // 8) * 8

decay_rate = 0.95
coef_a = 3.4445
coef_b = -4.775
coef_c = 2.0315
FINAL_SCALE = 0.2 * math.sqrt(max(ROWS, COLS))

bf16, f32 = jnp.bfloat16, jnp.float32


def place():
    d = lax.axis_index("dp")
    g = lax.axis_index("group")
    return d // (NYH * NZ), (d // NZ) % NYH, d % NZ, g // NC, g % NC


def dp_index(x, yh, z):
    return x * (NYH * NZ) + yh * NZ + z


def normalized(block):
    full = block.astype(f32)
    norm = jnp.sqrt(jnp.sum(jnp.sum(full * full, axis=1, keepdims=True), axis=0, keepdims=True))
    return (full * (1.0 / (norm + 1e-07))).astype(bf16)


def poly_of(here):
    gram = lax.dot_general(here, here, (((1,), (1,)), ((), ())), preferred_element_type=f32).astype(bf16)
    square = jnp.dot(gram, gram, preferred_element_type=f32)
    return (coef_b * gram.astype(f32) + coef_c * square).astype(bf16)


def stepped(here):
    return coef_a * here.astype(f32) + jnp.dot(poly_of(here), here, preferred_element_type=f32)


def comm_kernel(p_ref, m_ref, x1_ref, y0_ref, mo_ref, x0_ref, own_a, own_b, got_a, got_b, sum_a, sum_b, got_a2, got_b2,
                all_a, all_b, m_out, m_got, m_pair, m_a, m_b, q_got, lsem, ssem, rsem):
    x, yh, z, yl, core = place()
    xs = (x0_ref, x1_ref)
    counter = [0]

    def wrap(v, n):
        return lax.rem(v, n)

    sent = []

    def send(src, dst, device):
        i = counter[0]
        counter[0] += 1
        copy = pltpu.make_async_remote_copy(
            src_ref=src, dst_ref=dst, send_sem=ssem.at[i], recv_sem=rsem.at[i],
            device_id=device, device_id_type=MESH)
        copy.start()
        sent.append(copy)
        return copy

    x_peers = list(range(1, NX))
    z_peers = sorted(range(1, NZ), key=lambda d: -min(d, NZ - d))
    y_peers = list(range(1, NYH * NYL))
    yz_peers = [(dy, dz) for dy in range(NYH) for dz in range(NZ) if (dy, dz) != (0, 0)][::-1]
    xy_peers = [(dx, dy) for dx in range(NX) for dy in range(NYH) if (dx, dy) != (0, 0)][::-1]
    xc_peers = [(dx, dc) for dx in range(NX) for dc in range(NC) if (dx, dc) != (0, 0)]

    def at_z(dz):
        return {"dp": dp_index(x, yh, wrap(z + dz, NZ))}

    def at_x(dx):
        return {"dp": dp_index(wrap(x + dx, NX), yh, z)}

    def at_yz(t):
        return {"dp": dp_index(x, wrap(yh + t[0], NYH), wrap(z + t[1], NZ))}

    def at_xy(t):
        return {"dp": dp_index(wrap(x + t[0], NX), wrap(yh + t[1], NYH), z)}

    def at_xc(t):
        return {"group": yl * NC + wrap(core + t[1], NC), "dp": dp_index(wrap(x + t[0], NX), yh, z)}

    def at_y(dy):
        y = wrap(yh * NYL + yl + dy, NYH * NYL)
        return {"group": lax.rem(y, NYL) * NC + core, "dp": dp_index(x, y // NYL, z)}

    def cols_of(zz):
        return pl.ds(pl.multiple_of(zz * WIDE, WIDE), WIDE)

    own_cols = cols_of(z)

    local_a = pltpu.make_async_copy(p_ref.at[:, x, :, 0:TOP, :], own_a, lsem.at[0])
    local_b = pltpu.make_async_copy(p_ref.at[:, :, :, TOP:SLAB, own_cols], own_b, lsem.at[1])
    local_a.start()
    local_b.start()

    targets = [at_z(dz) for dz in z_peers] + [at_y(dy) for dy in y_peers] + [at_x(dx) for dx in x_peers]
    targets.append(at_xc((0, 1)))
    barrier = pltpu.get_barrier_semaphore()
    for device in targets:
        pl.semaphore_signal(barrier, inc=1, device_id=device, device_id_type=MESH)
    m_out[...] = jnp.zeros_like(m_out)
    for m in range(MATS):
        m_out[m, 0:OWN, :] = m_ref[:, m, :]
    m_got[z] = m_out[:, :, own_cols]
    pl.semaphore_wait(barrier, len(targets))

    m1 = [send(m_out.at[:, :, cols_of(wrap(z + dz, NZ))], m_got.at[z], at_z(dz)) for dz in z_peers]
    a1 = [[], []]
    b1 = []
    b_order = list(z_peers)

    def send_b():
        dz = b_order.pop(0)
        b1.append(send(p_ref.at[:, :, :, TOP:SLAB, cols_of(wrap(z + dz, NZ))], got_b.at[dz - 1], at_z(dz)))

    for m in range(MATS):
        for dx in x_peers:
            a1[m].append(send(p_ref.at[m, wrap(x + dx, NX), :, 0:TOP, :], got_a.at[m, dx - 1], at_x(dx)))
            if b_order:
                send_b()
    while b_order:
        send_b()

    row = lax.broadcasted_iota(jnp.int32, (SLAB, NZ * OWN_PAD), 0)
    slot = lax.broadcasted_iota(jnp.int32, (SLAB, NZ * OWN_PAD), 1)
    pick = ((slot // OWN_PAD) * OWN + slot % OWN_PAD == row) & (slot % OWN_PAD < OWN)
    pick = pick.astype(f32).astype(bf16)
    for copy in m1:
        copy.wait_recv()
    for m in range(MATS):
        block = jnp.dot(pick, m_got[:, m].reshape(NZ * OWN_PAD, WIDE).astype(bf16),
                        preferred_element_type=f32).astype(bf16)
        m_pair[m, yh] = block[0:TOP]
        m_b[m, x, yh] = block[TOP:SLAB]
    m2 = send(m_pair.at[:, yh], m_pair.at[:, yh], at_yz((1, 0)))

    local_a.wait()
    local_b.wait()
    a2 = []
    for m in range(MATS):
        for copy in a1[m]:
            copy.wait_recv()
        total = own_a[m].astype(f32)
        for j in range(NX - 1):
            total = total + got_a[m, j].astype(f32)
        sum_a[m] = total.astype(bf16)
        a2 += [send(sum_a.at[m, wrap(yh + t[0], NYH), :, cols_of(wrap(z + t[1], NZ))], got_a2.at[j, m], at_yz(t))
               for j, t in enumerate(yz_peers)]
    for copy in b1:
        copy.wait_recv()
    total = own_b[...].astype(f32)
    for j in range(NZ - 1):
        total = total + got_b[j].astype(f32)
    sum_b[...] = total.astype(bf16)
    b2 = [send(sum_b.at[:, wrap(x + t[0], NX), wrap(yh + t[1], NYH)], got_b2.at[j], at_xy(t))
          for j, t in enumerate(xy_peers)]

    m4 = [send(m_b.at[:, x, yh], m_b.at[:, x, yh], at_xy(t)) for t in xy_peers]
    m2.wait_recv()
    m_a[:, :, :, own_cols] = m_pair[...]

    def hop(t, before):
        for copy in before:
            copy.wait_recv()
        copies = []
        p = m_a.at[:, :, :, cols_of(wrap(z + NZ - t + 1, NZ))]
        copies.append(send(p, p, at_z(1)))
        if t < NZ // 2:
            n = m_a.at[:, :, :, cols_of(wrap(z + t - 1, NZ))]
            copies.append(send(n, n, at_z(NZ - 1)))
        return copies

    h1 = hop(1, [])
    for copy in a2:
        copy.wait_recv()
    top = sum_a[:, yh, :, own_cols].astype(f32)
    for j in range(len(yz_peers)):
        top = top + got_a2[j].astype(f32)
    h2 = hop(2, h1)
    for copy in b2:
        copy.wait_recv()
    rest = sum_b[:, x, yh].astype(f32)
    for j in range(len(xy_peers)):
        rest = rest + got_b2[j].astype(f32)

    square = jnp.zeros((8, WIDE), f32)
    for m in range(MATS):
        for part in (top[m], rest[m]):
            for r in range(0, part.shape[0], 8):
                square = square + part[r:r + 8] * part[r:r + 8]

    def spread(stage, mine, peers, at):
        q_got[stage, mine] = square
        here = q_got.at[stage, mine]
        return [send(here, here, at(t)) for t in peers]

    def gather(stage, copies):
        for copy in copies:
            copy.wait_recv()
        total = q_got[stage, 0]
        for j in range(1, len(copies) + 1):
            total = total + q_got[stage, j]
        return total

    q = spread(0, z, z_peers, at_z)
    all_a[:, yh, :, own_cols] = top.astype(bf16)
    all_b[:, x, yh] = rest.astype(bf16)
    here = all_a.at[:, yh, :, own_cols]
    pair = send(here, here, at_yz((1, 0)))
    here = all_b.at[:, x, yh]
    b3 = [send(here, here, at_xy(t)) for t in xy_peers]
    h3 = hop(3, h2)
    square = gather(0, q)
    q = spread(1, x * NC + core, xc_peers, at_xc)
    pair.wait_recv()
    here = all_a.at[:, :, :, own_cols]
    a3 = [send(here, here, at_z(dz)) for dz in z_peers]
    square = gather(1, q)
    q = spread(2, yh * NYL + yl, y_peers, at_y)
    h4 = hop(4, h3)
    m3 = h4
    square = gather(2, q)
    square_sum = jnp.sum(jnp.sum(square, axis=1, keepdims=True), axis=0, keepdims=True)
    entries = GROUPS * MATS * ROWS * COLS
    clip = jnp.minimum(1.0, math.sqrt(entries) / jnp.sqrt(square_sum + 1e-06))
    scale = (1.0 + decay_rate) * clip

    for copy in m3 + a3:
        copy.wait_recv()
    a4 = []
    b4 = []
    for m in range(MATS):
        for j in range(NYH):
            xs[m][x, j, 0:TOP, :] = (
                scale * all_a[m, j].astype(f32) + (decay_rate * decay_rate) * m_a[m, j].astype(f32)).astype(bf16)
        strip = xs[m].at[x, :, 0:TOP, :]
        a4.append([send(strip, strip, at_x(dx)) for dx in x_peers])
        if m == 0:
            for copy in m4 + b3:
                copy.wait_recv()
        for i in range(NX):
            for j in range(NYH):
                xs[m][i, j, TOP:SLAB, own_cols] = (
                    scale * all_b[m, i, j].astype(f32)
                    + (decay_rate * decay_rate) * m_b[m, i, j].astype(f32)).astype(bf16)
        strip = xs[m].at[:, :, TOP:SLAB, own_cols]
        b4.append([send(strip, strip, at_z(dz)) for dz in z_peers])

    for copy in a4[0] + b4[0]:
        copy.wait_recv()
    y0_ref[...] = normalized(x0_ref[...].reshape(ROWS, COLS))
    for _ in range(ITERS - 1):
        y0_ref[...] = stepped(y0_ref[...]).astype(bf16)
    y0_ref[...] = (stepped(y0_ref[...]) * FINAL_SCALE).astype(bf16)

    for copy in a4[1] + b4[1]:
        copy.wait_recv()

    row = lax.broadcasted_iota(jnp.int32, (OWN_PAD, SLAB), 0)
    col = lax.broadcasted_iota(jnp.int32, (OWN_PAD, SLAB), 1)
    pick = ((col == z * OWN + row) & (row < OWN)).astype(f32).astype(bf16)
    for m in range(MATS):
        mine = jnp.dot(pick, xs[m][x, yh], preferred_element_type=f32)[0:OWN]
        old = m_ref[:, m, :]
        grad = (mine - (decay_rate * decay_rate) * old) * (1.0 / (1.0 + decay_rate))
        mo_ref[:, m, :] = decay_rate * old + grad
    for copy in sent:
        copy.wait_send()


def comm(partials, momentum):
    z_n, yz_n, xy_n = NZ - 1, NYH * NZ - 1, NX * NYH - 1
    n_copies = 4 * (NX - 1) + 3 * z_n + 3 * yz_n + 2 * xy_n + 2 * z_n + xy_n + 1 + z_n + (NX * NC - 1) + (NYH * NYL - 1)
    return pl.pallas_call(
        comm_kernel,
        name="reduce_blend_gather",
        out_shape=(jax.ShapeDtypeStruct((NX, NYH, SLAB, COLS), bf16), jax.ShapeDtypeStruct((ROWS, COLS), bf16),
                   jax.ShapeDtypeStruct((OWN, MATS, COLS), f32)),
        in_specs=[pl.BlockSpec(memory_space=pltpu.HBM), pl.BlockSpec(memory_space=pltpu.VMEM)],
        out_specs=(pl.BlockSpec(memory_space=pltpu.VMEM),) * 3,
        scratch_shapes=[
            pltpu.VMEM((NX, NYH, SLAB, COLS), bf16),
            pltpu.VMEM((MATS, NYH, TOP, COLS), bf16),
            pltpu.VMEM((MATS, NX, NYH, REST, WIDE), bf16),
            pltpu.VMEM((MATS, NX - 1, NYH, TOP, COLS), bf16),
            pltpu.VMEM((NZ - 1, MATS, NX, NYH, REST, WIDE), bf16),
            pltpu.VMEM((MATS, NYH, TOP, COLS), bf16),
            pltpu.VMEM((MATS, NX, NYH, REST, WIDE), bf16),
            pltpu.VMEM((NYH * NZ - 1, MATS, TOP, WIDE), bf16),
            pltpu.VMEM((NX * NYH - 1, MATS, REST, WIDE), bf16),
            pltpu.VMEM((MATS, NYH, TOP, COLS), bf16),
            pltpu.VMEM((MATS, NX, NYH, REST, WIDE), bf16),
            pltpu.VMEM((MATS, OWN_PAD, COLS), f32),
            pltpu.VMEM((NZ, MATS, OWN_PAD, WIDE), f32),
            pltpu.VMEM((MATS, NYH, TOP, WIDE), bf16),
            pltpu.VMEM((MATS, NYH, TOP, COLS), bf16),
            pltpu.VMEM((MATS, NX, NYH, REST, WIDE), bf16),
            pltpu.VMEM((3, 8, 8, WIDE), f32),
            pltpu.SemaphoreType.DMA((2,)),
            pltpu.SemaphoreType.DMA((n_copies,)),
            pltpu.SemaphoreType.DMA((n_copies,)),
        ],
        compiler_params=pltpu.CompilerParams(
            collective_id=0, has_side_effects=True, vmem_limit_bytes=52 << 20),
        cost_estimate=pl.CostEstimate(flops=2_900_000_000, bytes_accessed=8_000_000, transcendentals=0),
    )(partials, momentum)


def newton_kernel(x1_ref, y0_ref, mi_ref, u_ref, mo_ref, cur, sem):
    copies = [pltpu.make_async_copy(y0_ref, u_ref.at[0], sem.at[0])]
    copies[0].start()
    mo_ref[...] = mi_ref[...]
    here = normalized(x1_ref[...].reshape(ROWS, COLS))
    for _ in range(ITERS - 1):
        here = stepped(here).astype(bf16)
    poly = poly_of(here)
    for i in range(PIECES):
        cols = slice(i * COLS // PIECES, (i + 1) * COLS // PIECES)
        part = here[:, cols]
        last = coef_a * part.astype(f32) + jnp.dot(poly, part, preferred_element_type=f32)
        cur[:, cols] = (last * FINAL_SCALE).astype(bf16)
        copies.append(pltpu.make_async_copy(cur.at[:, cols], u_ref.at[1, :, cols], sem.at[1 + i]))
        copies[-1].start()
    for copy in copies:
        copy.wait()


def newton(x1, y0, momentum_out):
    vmem = pl.BlockSpec(memory_space=pltpu.VMEM)
    return pl.pallas_call(
        newton_kernel,
        name="newton_schulz",
        out_shape=(jax.ShapeDtypeStruct((MATS, ROWS, COLS), bf16), jax.ShapeDtypeStruct((OWN, MATS, COLS), f32)),
        in_specs=[vmem, vmem, vmem],
        out_specs=(pl.BlockSpec(memory_space=pltpu.HBM), vmem),
        scratch_shapes=[pltpu.VMEM((ROWS, COLS), bf16), pltpu.SemaphoreType.DMA((1 + PIECES,))],
        compiler_params=pltpu.CompilerParams(vmem_limit_bytes=40 << 20),
        cost_estimate=pl.CostEstimate(flops=4_300_000_000, bytes_accessed=3_200_000, transcendentals=0),
    )(x1, y0, momentum_out)


def shards(partials, momentum):
    parts = partials.reshape(MATS, NX, NYH, SLAB, COLS)
    old = jnp.transpose(momentum[0], (1, 0, 2))
    update, momentum_out = newton(*comm(parts, old))
    return update[None], jnp.transpose(momentum_out, (1, 0, 2))[None]


def solution(mesh):
    in_specs = (P("group", "dp", None, None, None), P("group", None, "dp", None))
    out_specs = (P("group", None, None, None), P("group", None, "dp", None))
    return jax.shard_map(shards, mesh=mesh, in_specs=in_specs, out_specs=out_specs, check_vma=False)
```

```python
import functools
import math

import jax
import jax.numpy as jnp
from jax import lax
from jax.experimental import pallas as pl
from jax.experimental.pallas import tpu as pltpu
from jax.sharding import PartitionSpec as P

MESH = pl.DeviceIdType.MESH

MATS = 2
ROWS = 384
COLS = 1024
ITERS = 5
PIECES = 2
GROUPS = 8

NX, NYH, NZ, NYL, NC = 4, 2, 8, 4, 2
SLAB = ROWS // (NX * NYH)
WIDE = COLS // NZ
TOP = SLAB * 2 // 3
REST = SLAB - TOP
OWN = SLAB // NZ
OWN_PAD = -(-OWN // 8) * 8

decay_rate = 0.95
coef_a = 3.4445
coef_b = -4.775
coef_c = 2.0315
FINAL_SCALE = 0.2 * math.sqrt(max(ROWS, COLS))

bf16, f32 = jnp.bfloat16, jnp.float32


def place():
    d = lax.axis_index("dp")
    g = lax.axis_index("group")
    return d // (NYH * NZ), (d // NZ) % NYH, d % NZ, g // NC, g % NC


def dp_index(x, yh, z):
    return x * (NYH * NZ) + yh * NZ + z


def normalized(block):
    full = block.astype(f32)
    norm = jnp.sqrt(jnp.sum(jnp.sum(full * full, axis=1, keepdims=True), axis=0, keepdims=True))
    return (full * (1.0 / (norm + 1e-07))).astype(bf16)


def poly_of(here):
    gram = lax.dot_general(here, here, (((1,), (1,)), ((), ())), preferred_element_type=f32).astype(bf16)
    square = jnp.dot(gram, gram, preferred_element_type=f32)
    return (coef_b * gram.astype(f32) + coef_c * square).astype(bf16)


def stepped(here):
    return coef_a * here.astype(f32) + jnp.dot(poly_of(here), here, preferred_element_type=f32)


def comm_kernel(p_ref, m_ref, x1_ref, y0_ref, mo_ref, x0_ref, own_a, own_b, got_a, got_b, sum_a, sum_b, got_a2, got_b2,
                all_a, all_b, m_out, m_got, m_pair, m_a, m_b, q_got, lsem, ssem, rsem):
    x, yh, z, yl, core = place()
    xs = (x0_ref, x1_ref)
    counter = [0]

    def wrap(v, n):
        return lax.rem(v, n)

    sent = []

    def send(src, dst, device):
        i = counter[0]
        counter[0] += 1
        copy = pltpu.make_async_remote_copy(
            src_ref=src, dst_ref=dst, send_sem=ssem.at[i], recv_sem=rsem.at[i],
            device_id=device, device_id_type=MESH)
        copy.start()
        sent.append(copy)
        return copy

    x_peers = sorted(range(1, NX), key=lambda d: -min(d, NX - d))
    z_peers = sorted(range(1, NZ), key=lambda d: -min(d, NZ - d))
    y_peers = list(range(1, NYH * NYL))
    yz_peers = [(dy, dz) for dy in range(NYH) for dz in range(NZ) if (dy, dz) != (0, 0)][::-1]
    xy_peers = [(dx, dy) for dx in range(NX) for dy in range(NYH) if (dx, dy) != (0, 0)][::-1]
    xc_peers = [(dx, dc) for dx in range(NX) for dc in range(NC) if (dx, dc) != (0, 0)]

    def at_z(dz):
        return {"dp": dp_index(x, yh, wrap(z + dz, NZ))}

    def at_x(dx):
        return {"dp": dp_index(wrap(x + dx, NX), yh, z)}

    def at_yz(t):
        return {"dp": dp_index(x, wrap(yh + t[0], NYH), wrap(z + t[1], NZ))}

    def at_xy(t):
        return {"dp": dp_index(wrap(x + t[0], NX), wrap(yh + t[1], NYH), z)}

    def at_xc(t):
        return {"group": yl * NC + wrap(core + t[1], NC), "dp": dp_index(wrap(x + t[0], NX), yh, z)}

    def at_y(dy):
        y = wrap(yh * NYL + yl + dy, NYH * NYL)
        return {"group": lax.rem(y, NYL) * NC + core, "dp": dp_index(x, y // NYL, z)}

    def cols_of(zz):
        return pl.ds(pl.multiple_of(zz * WIDE, WIDE), WIDE)

    own_cols = cols_of(z)

    local_a = pltpu.make_async_copy(p_ref.at[:, x, :, 0:TOP, :], own_a, lsem.at[0])
    local_b = pltpu.make_async_copy(p_ref.at[:, :, :, TOP:SLAB, own_cols], own_b, lsem.at[1])
    local_a.start()
    local_b.start()

    targets = [at_z(dz) for dz in z_peers] + [at_y(dy) for dy in y_peers] + [at_x(dx) for dx in x_peers]
    targets.append(at_xc((0, 1)))
    barrier = pltpu.get_barrier_semaphore()
    for device in targets:
        pl.semaphore_signal(barrier, inc=1, device_id=device, device_id_type=MESH)
    m_out[...] = jnp.zeros_like(m_out)
    for m in range(MATS):
        m_out[m, 0:OWN, :] = m_ref[:, m, :]
    m_got[z] = m_out[:, :, own_cols]
    pl.semaphore_wait(barrier, len(targets))

    m1 = [send(m_out.at[:, :, cols_of(wrap(z + dz, NZ))], m_got.at[z], at_z(dz)) for dz in z_peers]
    a1 = [[], []]
    b1 = []
    b_order = list(z_peers)

    def send_b():
        dz = b_order.pop(0)
        b1.append(send(p_ref.at[:, :, :, TOP:SLAB, cols_of(wrap(z + dz, NZ))], got_b.at[dz - 1], at_z(dz)))

    for m in range(MATS):
        for dx in x_peers:
            a1[m].append(send(p_ref.at[m, wrap(x + dx, NX), :, 0:TOP, :], got_a.at[m, dx - 1], at_x(dx)))
            if b_order:
                send_b()
    while b_order:
        send_b()

    row = lax.broadcasted_iota(jnp.int32, (SLAB, NZ * OWN_PAD), 0)
    slot = lax.broadcasted_iota(jnp.int32, (SLAB, NZ * OWN_PAD), 1)
    pick = ((slot // OWN_PAD) * OWN + slot % OWN_PAD == row) & (slot % OWN_PAD < OWN)
    pick = pick.astype(f32).astype(bf16)
    for copy in m1:
        copy.wait_recv()
    for m in range(MATS):
        block = jnp.dot(pick, m_got[:, m].reshape(NZ * OWN_PAD, WIDE).astype(bf16),
                        preferred_element_type=f32).astype(bf16)
        m_pair[m, yh] = block[0:TOP]
        m_b[m, x, yh] = block[TOP:SLAB]
    m2 = send(m_pair.at[:, yh], m_pair.at[:, yh], at_yz((1, 0)))

    local_a.wait()
    local_b.wait()
    a2 = []
    for m in range(MATS):
        for copy in a1[m]:
            copy.wait_recv()
        total = own_a[m].astype(f32)
        for j in range(NX - 1):
            total = total + got_a[m, j].astype(f32)
        sum_a[m] = total.astype(bf16)
        a2 += [send(sum_a.at[m, wrap(yh + t[0], NYH), :, cols_of(wrap(z + t[1], NZ))], got_a2.at[j, m], at_yz(t))
               for j, t in enumerate(yz_peers)]
    for copy in b1:
        copy.wait_recv()
    total = own_b[...].astype(f32)
    for j in range(NZ - 1):
        total = total + got_b[j].astype(f32)
    sum_b[...] = total.astype(bf16)
    b2 = [send(sum_b.at[:, wrap(x + t[0], NX), wrap(yh + t[1], NYH)], got_b2.at[j], at_xy(t))
          for j, t in enumerate(xy_peers)]

    m4 = [send(m_b.at[:, x, yh], m_b.at[:, x, yh], at_xy(t)) for t in xy_peers]
    m2.wait_recv()
    m_a[:, :, :, own_cols] = m_pair[...]

    def hop(t, before):
        for copy in before:
            copy.wait_recv()
        copies = []
        p = m_a.at[:, :, :, cols_of(wrap(z + NZ - t + 1, NZ))]
        copies.append(send(p, p, at_z(1)))
        if t < NZ // 2:
            n = m_a.at[:, :, :, cols_of(wrap(z + t - 1, NZ))]
            copies.append(send(n, n, at_z(NZ - 1)))
        return copies

    h1 = hop(1, [])
    for copy in a2:
        copy.wait_recv()
    top = sum_a[:, yh, :, own_cols].astype(f32)
    for j in range(len(yz_peers)):
        top = top + got_a2[j].astype(f32)
    h2 = hop(2, h1)
    for copy in b2:
        copy.wait_recv()
    rest = sum_b[:, x, yh].astype(f32)
    for j in range(len(xy_peers)):
        rest = rest + got_b2[j].astype(f32)

    square = jnp.zeros((8, WIDE), f32)
    for m in range(MATS):
        for part in (top[m], rest[m]):
            for r in range(0, part.shape[0], 8):
                square = square + part[r:r + 8] * part[r:r + 8]

    def spread(stage, mine, peers, at):
        q_got[stage, mine] = square
        here = q_got.at[stage, mine]
        return [send(here, here, at(t)) for t in peers]

    def gather(stage, copies):
        for copy in copies:
            copy.wait_recv()
        total = q_got[stage, 0]
        for j in range(1, len(copies) + 1):
            total = total + q_got[stage, j]
        return total

    q = spread(0, z, z_peers, at_z)
    all_a[:, yh, :, own_cols] = top.astype(bf16)
    all_b[:, x, yh] = rest.astype(bf16)
    here = all_a.at[:, yh, :, own_cols]
    pair = send(here, here, at_yz((1, 0)))
    here = all_b.at[:, x, yh]
    b3 = [send(here, here, at_xy(t)) for t in xy_peers]
    h3 = hop(3, h2)
    square = gather(0, q)
    q = spread(1, x * NC + core, xc_peers, at_xc)
    pair.wait_recv()
    here = all_a.at[:, :, :, own_cols]
    a3 = [send(here, here, at_z(dz)) for dz in z_peers]
    square = gather(1, q)
    q = spread(2, yh * NYL + yl, y_peers, at_y)
    h4 = hop(4, h3)
    m3 = h4
    square = gather(2, q)
    square_sum = jnp.sum(jnp.sum(square, axis=1, keepdims=True), axis=0, keepdims=True)
    entries = GROUPS * MATS * ROWS * COLS
    clip = jnp.minimum(1.0, math.sqrt(entries) / jnp.sqrt(square_sum + 1e-06))
    scale = (1.0 + decay_rate) * clip

    for copy in m4 + b3:
        copy.wait_recv()
    a4 = []
    b4 = []
    for m in range(MATS):
        for i in range(NX):
            for j in range(NYH):
                xs[m][i, j, TOP:SLAB, own_cols] = (
                    scale * all_b[m, i, j].astype(f32)
                    + (decay_rate * decay_rate) * m_b[m, i, j].astype(f32)).astype(bf16)
        strip = xs[m].at[:, :, TOP:SLAB, own_cols]
        b4.append([send(strip, strip, at_z(dz)) for dz in z_peers])
        if m == 0:
            for copy in m3 + a3:
                copy.wait_recv()
        for j in range(NYH):
            xs[m][x, j, 0:TOP, :] = (
                scale * all_a[m, j].astype(f32) + (decay_rate * decay_rate) * m_a[m, j].astype(f32)).astype(bf16)
        strip = xs[m].at[x, :, 0:TOP, :]
        a4.append([send(strip, strip, at_x(dx)) for dx in x_peers])

    for copy in a4[0] + b4[0]:
        copy.wait_recv()
    y0_ref[...] = normalized(x0_ref[...].reshape(ROWS, COLS))
    for _ in range(ITERS - 1):
        y0_ref[...] = stepped(y0_ref[...]).astype(bf16)
    y0_ref[...] = (stepped(y0_ref[...]) * FINAL_SCALE).astype(bf16)

    for copy in a4[1] + b4[1]:
        copy.wait_recv()

    row = lax.broadcasted_iota(jnp.int32, (OWN_PAD, SLAB), 0)
    col = lax.broadcasted_iota(jnp.int32, (OWN_PAD, SLAB), 1)
    pick = ((col == z * OWN + row) & (row < OWN)).astype(f32).astype(bf16)
    for m in range(MATS):
        mine = jnp.dot(pick, xs[m][x, yh], preferred_element_type=f32)[0:OWN]
        old = m_ref[:, m, :]
        grad = (mine - (decay_rate * decay_rate) * old) * (1.0 / (1.0 + decay_rate))
        mo_ref[:, m, :] = decay_rate * old + grad
    for copy in sent:
        copy.wait_send()


def comm(partials, momentum):
    z_n, yz_n, xy_n = NZ - 1, NYH * NZ - 1, NX * NYH - 1
    n_copies = 4 * (NX - 1) + 3 * z_n + 3 * yz_n + 2 * xy_n + 2 * z_n + xy_n + 1 + z_n + (NX * NC - 1) + (NYH * NYL - 1)
    return pl.pallas_call(
        comm_kernel,
        name="reduce_blend_gather",
        out_shape=(jax.ShapeDtypeStruct((NX, NYH, SLAB, COLS), bf16), jax.ShapeDtypeStruct((ROWS, COLS), bf16),
                   jax.ShapeDtypeStruct((OWN, MATS, COLS), f32)),
        in_specs=[pl.BlockSpec(memory_space=pltpu.HBM), pl.BlockSpec(memory_space=pltpu.VMEM)],
        out_specs=(pl.BlockSpec(memory_space=pltpu.VMEM),) * 3,
        scratch_shapes=[
            pltpu.VMEM((NX, NYH, SLAB, COLS), bf16),
            pltpu.VMEM((MATS, NYH, TOP, COLS), bf16),
            pltpu.VMEM((MATS, NX, NYH, REST, WIDE), bf16),
            pltpu.VMEM((MATS, NX - 1, NYH, TOP, COLS), bf16),
            pltpu.VMEM((NZ - 1, MATS, NX, NYH, REST, WIDE), bf16),
            pltpu.VMEM((MATS, NYH, TOP, COLS), bf16),
            pltpu.VMEM((MATS, NX, NYH, REST, WIDE), bf16),
            pltpu.VMEM((NYH * NZ - 1, MATS, TOP, WIDE), bf16),
            pltpu.VMEM((NX * NYH - 1, MATS, REST, WIDE), bf16),
            pltpu.VMEM((MATS, NYH, TOP, COLS), bf16),
            pltpu.VMEM((MATS, NX, NYH, REST, WIDE), bf16),
            pltpu.VMEM((MATS, OWN_PAD, COLS), f32),
            pltpu.VMEM((NZ, MATS, OWN_PAD, WIDE), f32),
            pltpu.VMEM((MATS, NYH, TOP, WIDE), bf16),
            pltpu.VMEM((MATS, NYH, TOP, COLS), bf16),
            pltpu.VMEM((MATS, NX, NYH, REST, WIDE), bf16),
            pltpu.VMEM((3, 8, 8, WIDE), f32),
            pltpu.SemaphoreType.DMA((2,)),
            pltpu.SemaphoreType.DMA((n_copies,)),
            pltpu.SemaphoreType.DMA((n_copies,)),
        ],
        compiler_params=pltpu.CompilerParams(
            collective_id=0, has_side_effects=True, vmem_limit_bytes=52 << 20),
        cost_estimate=pl.CostEstimate(flops=2_900_000_000, bytes_accessed=8_000_000, transcendentals=0),
    )(partials, momentum)


def newton_kernel(x1_ref, y0_ref, mi_ref, u_ref, mo_ref, cur, sem):
    copies = [pltpu.make_async_copy(y0_ref, u_ref.at[0], sem.at[0])]
    copies[0].start()
    mo_ref[...] = mi_ref[...]
    here = normalized(x1_ref[...].reshape(ROWS, COLS))
    for _ in range(ITERS - 1):
        here = stepped(here).astype(bf16)
    poly = poly_of(here)
    for i in range(PIECES):
        cols = slice(i * COLS // PIECES, (i + 1) * COLS // PIECES)
        part = here[:, cols]
        last = coef_a * part.astype(f32) + jnp.dot(poly, part, preferred_element_type=f32)
        cur[:, cols] = (last * FINAL_SCALE).astype(bf16)
        copies.append(pltpu.make_async_copy(cur.at[:, cols], u_ref.at[1, :, cols], sem.at[1 + i]))
        copies[-1].start()
    for copy in copies:
        copy.wait()


def newton(x1, y0, momentum_out):
    vmem = pl.BlockSpec(memory_space=pltpu.VMEM)
    return pl.pallas_call(
        newton_kernel,
        name="newton_schulz",
        out_shape=(jax.ShapeDtypeStruct((MATS, ROWS, COLS), bf16), jax.ShapeDtypeStruct((OWN, MATS, COLS), f32)),
        in_specs=[vmem, vmem, vmem],
        out_specs=(pl.BlockSpec(memory_space=pltpu.HBM), vmem),
        scratch_shapes=[pltpu.VMEM((ROWS, COLS), bf16), pltpu.SemaphoreType.DMA((1 + PIECES,))],
        compiler_params=pltpu.CompilerParams(vmem_limit_bytes=40 << 20),
        cost_estimate=pl.CostEstimate(flops=4_300_000_000, bytes_accessed=3_200_000, transcendentals=0),
    )(x1, y0, momentum_out)


def shards(partials, momentum):
    parts = partials.reshape(MATS, NX, NYH, SLAB, COLS)
    old = jnp.transpose(momentum[0], (1, 0, 2))
    update, momentum_out = newton(*comm(parts, old))
    return update[None], jnp.transpose(momentum_out, (1, 0, 2))[None]


def solution(mesh):
    in_specs = (P("group", "dp", None, None, None), P("group", None, "dp", None))
    out_specs = (P("group", None, None, None), P("group", None, "dp", None))
    return jax.shard_map(shards, mesh=mesh, in_specs=in_specs, out_specs=out_specs, check_vma=False)
```

```python
import functools
import math

import jax
import jax.numpy as jnp
from jax import lax
from jax.experimental import pallas as pl
from jax.experimental.pallas import tpu as pltpu
from jax.sharding import PartitionSpec as P

MESH = pl.DeviceIdType.MESH

MATS = 2
ROWS = 384
COLS = 1024
ITERS = 5
EARLY = 3
PIECES = 2
GROUPS = 8

NX, NYH, NZ, NYL, NC = 4, 2, 8, 4, 2
SLAB = ROWS // (NX * NYH)
WIDE = COLS // NZ
TOP = SLAB * 2 // 3
REST = SLAB - TOP
OWN = SLAB // NZ
OWN_PAD = -(-OWN // 8) * 8

decay_rate = 0.95
coef_a = 3.4445
coef_b = -4.775
coef_c = 2.0315
FINAL_SCALE = 0.2 * math.sqrt(max(ROWS, COLS))

bf16, f32 = jnp.bfloat16, jnp.float32


def place():
    d = lax.axis_index("dp")
    g = lax.axis_index("group")
    return d // (NYH * NZ), (d // NZ) % NYH, d % NZ, g // NC, g % NC


def dp_index(x, yh, z):
    return x * (NYH * NZ) + yh * NZ + z


def normalized(block):
    full = block.astype(f32)
    norm = jnp.sqrt(jnp.sum(jnp.sum(full * full, axis=1, keepdims=True), axis=0, keepdims=True))
    return (full * (1.0 / (norm + 1e-07))).astype(bf16)


def poly_of(here):
    gram = lax.dot_general(here, here, (((1,), (1,)), ((), ())), preferred_element_type=f32).astype(bf16)
    square = jnp.dot(gram, gram, preferred_element_type=f32)
    return (coef_b * gram.astype(f32) + coef_c * square).astype(bf16)


def stepped(here):
    return coef_a * here.astype(f32) + jnp.dot(poly_of(here), here, preferred_element_type=f32)


def comm_kernel(p_ref, m_ref, x1_ref, y0_ref, mo_ref, x0_ref, own_a, own_b, got_a, got_b, sum_a, sum_b, got_a2, got_b2,
                all_a, all_b, m_out, m_got, m_pair, m_a, m_b, q_got, lsem, ssem, rsem):
    x, yh, z, yl, core = place()
    xs = (x0_ref, x1_ref)
    counter = [0]

    def wrap(v, n):
        return lax.rem(v, n)

    sent = []

    def send(src, dst, device):
        i = counter[0]
        counter[0] += 1
        copy = pltpu.make_async_remote_copy(
            src_ref=src, dst_ref=dst, send_sem=ssem.at[i], recv_sem=rsem.at[i],
            device_id=device, device_id_type=MESH)
        copy.start()
        sent.append(copy)
        return copy

    x_peers = list(range(1, NX))
    z_peers = sorted(range(1, NZ), key=lambda d: -min(d, NZ - d))
    y_peers = list(range(1, NYH * NYL))
    yz_peers = [(dy, dz) for dy in range(NYH) for dz in range(NZ) if (dy, dz) != (0, 0)][::-1]
    xy_peers = [(dx, dy) for dx in range(NX) for dy in range(NYH) if (dx, dy) != (0, 0)][::-1]
    xc_peers = [(dx, dc) for dx in range(NX) for dc in range(NC) if (dx, dc) != (0, 0)]

    def at_z(dz):
        return {"dp": dp_index(x, yh, wrap(z + dz, NZ))}

    def at_x(dx):
        return {"dp": dp_index(wrap(x + dx, NX), yh, z)}

    def at_yz(t):
        return {"dp": dp_index(x, wrap(yh + t[0], NYH), wrap(z + t[1], NZ))}

    def at_xy(t):
        return {"dp": dp_index(wrap(x + t[0], NX), wrap(yh + t[1], NYH), z)}

    def at_xc(t):
        return {"group": yl * NC + wrap(core + t[1], NC), "dp": dp_index(wrap(x + t[0], NX), yh, z)}

    def at_y(dy):
        y = wrap(yh * NYL + yl + dy, NYH * NYL)
        return {"group": lax.rem(y, NYL) * NC + core, "dp": dp_index(x, y // NYL, z)}

    def cols_of(zz):
        return pl.ds(pl.multiple_of(zz * WIDE, WIDE), WIDE)

    own_cols = cols_of(z)

    local_a = pltpu.make_async_copy(p_ref.at[:, x, :, 0:TOP, :], own_a, lsem.at[0])
    local_b = pltpu.make_async_copy(p_ref.at[:, :, :, TOP:SLAB, own_cols], own_b, lsem.at[1])
    local_a.start()
    local_b.start()

    targets = [at_z(dz) for dz in z_peers] + [at_y(dy) for dy in y_peers] + [at_x(dx) for dx in x_peers]
    targets.append(at_xc((0, 1)))
    barrier = pltpu.get_barrier_semaphore()
    for device in targets:
        pl.semaphore_signal(barrier, inc=1, device_id=device, device_id_type=MESH)
    m_out[...] = jnp.zeros_like(m_out)
    for m in range(MATS):
        m_out[m, 0:OWN, :] = m_ref[:, m, :]
    m_got[z] = m_out[:, :, own_cols]
    pl.semaphore_wait(barrier, len(targets))

    m1 = [send(m_out.at[:, :, cols_of(wrap(z + dz, NZ))], m_got.at[z], at_z(dz)) for dz in z_peers]
    a1 = [[], []]
    b1 = []
    b_order = list(z_peers)

    def send_b():
        dz = b_order.pop(0)
        b1.append(send(p_ref.at[:, :, :, TOP:SLAB, cols_of(wrap(z + dz, NZ))], got_b.at[dz - 1], at_z(dz)))

    for m in range(MATS):
        for dx in x_peers:
            a1[m].append(send(p_ref.at[m, wrap(x + dx, NX), :, 0:TOP, :], got_a.at[m, dx - 1], at_x(dx)))
            if b_order:
                send_b()
    while b_order:
        send_b()

    row = lax.broadcasted_iota(jnp.int32, (SLAB, NZ * OWN_PAD), 0)
    slot = lax.broadcasted_iota(jnp.int32, (SLAB, NZ * OWN_PAD), 1)
    pick = ((slot // OWN_PAD) * OWN + slot % OWN_PAD == row) & (slot % OWN_PAD < OWN)
    pick = pick.astype(f32).astype(bf16)
    for copy in m1:
        copy.wait_recv()
    for m in range(MATS):
        block = jnp.dot(pick, m_got[:, m].reshape(NZ * OWN_PAD, WIDE).astype(bf16),
                        preferred_element_type=f32).astype(bf16)
        m_pair[m, yh] = block[0:TOP]
        m_b[m, x, yh] = block[TOP:SLAB]
    m2 = send(m_pair.at[:, yh], m_pair.at[:, yh], at_yz((1, 0)))

    local_a.wait()
    local_b.wait()
    a2 = []
    for m in range(MATS):
        for copy in a1[m]:
            copy.wait_recv()
        total = own_a[m].astype(f32)
        for j in range(NX - 1):
            total = total + got_a[m, j].astype(f32)
        sum_a[m] = total.astype(bf16)
        a2 += [send(sum_a.at[m, wrap(yh + t[0], NYH), :, cols_of(wrap(z + t[1], NZ))], got_a2.at[j, m], at_yz(t))
               for j, t in enumerate(yz_peers)]
    for copy in b1:
        copy.wait_recv()
    total = own_b[...].astype(f32)
    for j in range(NZ - 1):
        total = total + got_b[j].astype(f32)
    sum_b[...] = total.astype(bf16)
    b2 = [send(sum_b.at[:, wrap(x + t[0], NX), wrap(yh + t[1], NYH)], got_b2.at[j], at_xy(t))
          for j, t in enumerate(xy_peers)]

    m4 = [send(m_b.at[:, x, yh], m_b.at[:, x, yh], at_xy(t)) for t in xy_peers]
    m2.wait_recv()
    m_a[:, :, :, own_cols] = m_pair[...]

    def hop(t, before):
        for copy in before:
            copy.wait_recv()
        copies = []
        p = m_a.at[:, :, :, cols_of(wrap(z + NZ - t + 1, NZ))]
        copies.append(send(p, p, at_z(1)))
        if t < NZ // 2:
            n = m_a.at[:, :, :, cols_of(wrap(z + t - 1, NZ))]
            copies.append(send(n, n, at_z(NZ - 1)))
        return copies

    h1 = hop(1, [])
    for copy in a2:
        copy.wait_recv()
    top = sum_a[:, yh, :, own_cols].astype(f32)
    for j in range(len(yz_peers)):
        top = top + got_a2[j].astype(f32)
    h2 = hop(2, h1)
    for copy in b2:
        copy.wait_recv()
    rest = sum_b[:, x, yh].astype(f32)
    for j in range(len(xy_peers)):
        rest = rest + got_b2[j].astype(f32)

    square = jnp.zeros((8, WIDE), f32)
    for m in range(MATS):
        for part in (top[m], rest[m]):
            for r in range(0, part.shape[0], 8):
                square = square + part[r:r + 8] * part[r:r + 8]

    def spread(stage, mine, peers, at):
        q_got[stage, mine] = square
        here = q_got.at[stage, mine]
        return [send(here, here, at(t)) for t in peers]

    def gather(stage, copies):
        for copy in copies:
            copy.wait_recv()
        total = q_got[stage, 0]
        for j in range(1, len(copies) + 1):
            total = total + q_got[stage, j]
        return total

    q = spread(0, z, z_peers, at_z)
    all_a[:, yh, :, own_cols] = top.astype(bf16)
    all_b[:, x, yh] = rest.astype(bf16)
    here = all_a.at[:, yh, :, own_cols]
    pair = send(here, here, at_yz((1, 0)))
    here = all_b.at[:, x, yh]
    b3 = [send(here, here, at_xy(t)) for t in xy_peers]
    h3 = hop(3, h2)
    square = gather(0, q)
    q = spread(1, x * NC + core, xc_peers, at_xc)
    pair.wait_recv()
    here = all_a.at[:, :, :, own_cols]
    a3 = [send(here, here, at_z(dz)) for dz in z_peers]
    square = gather(1, q)
    q = spread(2, yh * NYL + yl, y_peers, at_y)
    h4 = hop(4, h3)
    m3 = h4
    square = gather(2, q)
    square_sum = jnp.sum(jnp.sum(square, axis=1, keepdims=True), axis=0, keepdims=True)
    entries = GROUPS * MATS * ROWS * COLS
    clip = jnp.minimum(1.0, math.sqrt(entries) / jnp.sqrt(square_sum + 1e-06))
    scale = (1.0 + decay_rate) * clip

    for copy in m3 + a3:
        copy.wait_recv()
    a4 = []
    b4 = []
    for m in range(MATS):
        for j in range(NYH):
            xs[m][x, j, 0:TOP, :] = (
                scale * all_a[m, j].astype(f32) + (decay_rate * decay_rate) * m_a[m, j].astype(f32)).astype(bf16)
        strip = xs[m].at[x, :, 0:TOP, :]
        a4.append([send(strip, strip, at_x(dx)) for dx in x_peers])
        if m == 0:
            for copy in m4 + b3:
                copy.wait_recv()
        for i in range(NX):
            for j in range(NYH):
                xs[m][i, j, TOP:SLAB, own_cols] = (
                    scale * all_b[m, i, j].astype(f32)
                    + (decay_rate * decay_rate) * m_b[m, i, j].astype(f32)).astype(bf16)
        strip = xs[m].at[:, :, TOP:SLAB, own_cols]
        b4.append([send(strip, strip, at_z(dz)) for dz in z_peers])

    for copy in a4[0] + b4[0]:
        copy.wait_recv()
    y0_ref[...] = normalized(x0_ref[...].reshape(ROWS, COLS))
    for _ in range(EARLY):
        y0_ref[...] = stepped(y0_ref[...]).astype(bf16)

    for copy in a4[1] + b4[1]:
        copy.wait_recv()

    row = lax.broadcasted_iota(jnp.int32, (OWN_PAD, SLAB), 0)
    col = lax.broadcasted_iota(jnp.int32, (OWN_PAD, SLAB), 1)
    pick = ((col == z * OWN + row) & (row < OWN)).astype(f32).astype(bf16)
    for m in range(MATS):
        mine = jnp.dot(pick, xs[m][x, yh], preferred_element_type=f32)[0:OWN]
        old = m_ref[:, m, :]
        grad = (mine - (decay_rate * decay_rate) * old) * (1.0 / (1.0 + decay_rate))
        mo_ref[:, m, :] = decay_rate * old + grad
    for copy in sent:
        copy.wait_send()


def comm(partials, momentum):
    z_n, yz_n, xy_n = NZ - 1, NYH * NZ - 1, NX * NYH - 1
    n_copies = 4 * (NX - 1) + 3 * z_n + 3 * yz_n + 2 * xy_n + 2 * z_n + xy_n + 1 + z_n + (NX * NC - 1) + (NYH * NYL - 1)
    return pl.pallas_call(
        comm_kernel,
        name="reduce_blend_gather",
        out_shape=(jax.ShapeDtypeStruct((NX, NYH, SLAB, COLS), bf16), jax.ShapeDtypeStruct((ROWS, COLS), bf16),
                   jax.ShapeDtypeStruct((OWN, MATS, COLS), f32)),
        in_specs=[pl.BlockSpec(memory_space=pltpu.HBM), pl.BlockSpec(memory_space=pltpu.VMEM)],
        out_specs=(pl.BlockSpec(memory_space=pltpu.VMEM),) * 3,
        scratch_shapes=[
            pltpu.VMEM((NX, NYH, SLAB, COLS), bf16),
            pltpu.VMEM((MATS, NYH, TOP, COLS), bf16),
            pltpu.VMEM((MATS, NX, NYH, REST, WIDE), bf16),
            pltpu.VMEM((MATS, NX - 1, NYH, TOP, COLS), bf16),
            pltpu.VMEM((NZ - 1, MATS, NX, NYH, REST, WIDE), bf16),
            pltpu.VMEM((MATS, NYH, TOP, COLS), bf16),
            pltpu.VMEM((MATS, NX, NYH, REST, WIDE), bf16),
            pltpu.VMEM((NYH * NZ - 1, MATS, TOP, WIDE), bf16),
            pltpu.VMEM((NX * NYH - 1, MATS, REST, WIDE), bf16),
            pltpu.VMEM((MATS, NYH, TOP, COLS), bf16),
            pltpu.VMEM((MATS, NX, NYH, REST, WIDE), bf16),
            pltpu.VMEM((MATS, OWN_PAD, COLS), f32),
            pltpu.VMEM((NZ, MATS, OWN_PAD, WIDE), f32),
            pltpu.VMEM((MATS, NYH, TOP, WIDE), bf16),
            pltpu.VMEM((MATS, NYH, TOP, COLS), bf16),
            pltpu.VMEM((MATS, NX, NYH, REST, WIDE), bf16),
            pltpu.VMEM((3, 8, 8, WIDE), f32),
            pltpu.SemaphoreType.DMA((2,)),
            pltpu.SemaphoreType.DMA((n_copies,)),
            pltpu.SemaphoreType.DMA((n_copies,)),
        ],
        compiler_params=pltpu.CompilerParams(
            collective_id=0, has_side_effects=True, vmem_limit_bytes=52 << 20),
        cost_estimate=pl.CostEstimate(flops=2_900_000_000, bytes_accessed=8_000_000, transcendentals=0),
    )(partials, momentum)


def poly_by_halves(here, out):
    half = 256
    left = lax.dot_general(here, here[0:half], (((1,), (1,)), ((), ())), preferred_element_type=f32)
    corner = lax.dot_general(here[half:], here[half:], (((1,), (1,)), ((), ())), preferred_element_type=f32)
    for last in (False, True):
        out[:, 0:half] = left.astype(bf16)
        out[half:, half:] = corner.astype(bf16)
        out[0:half, half:] = left[half:].T.astype(bf16)
        gram = out[...]
        if last:
            return gram
        left = coef_b * gram[:, 0:half].astype(f32) + coef_c * jnp.dot(
            gram, gram[:, 0:half], preferred_element_type=f32)
        corner = coef_b * gram[half:, half:].astype(f32) + coef_c * jnp.dot(
            gram[half:], gram[:, half:], preferred_element_type=f32)


def newton_kernel(x1_ref, y0_ref, mi_ref, u_ref, mo_ref, cur, poly_buf, sem):
    mo_ref[...] = mi_ref[...]
    copies = []

    def write(m, i, cols, value):
        cur[m, :, cols] = (value * FINAL_SCALE).astype(bf16)
        copies.append(pltpu.make_async_copy(cur.at[m, :, cols], u_ref.at[m, :, cols], sem.at[i]))
        copies[-1].start()

    def advance(m, poly):
        here = cur[m]
        return coef_a * here.astype(f32) + jnp.dot(poly, here, preferred_element_type=f32)

    cur[0] = y0_ref[...]
    cur[1] = normalized(x1_ref[...].reshape(ROWS, COLS))
    pairs = ITERS - EARLY
    for t in range(pairs):
        polys = [poly_by_halves(cur[m], poly_buf.at[m]) for m in range(MATS)]
        value = advance(0, polys[0])
        if t + 1 < pairs:
            cur[0] = value.astype(bf16)
        else:
            write(0, 0, slice(0, COLS), value)
        cur[1] = advance(1, polys[1]).astype(bf16)
    for _ in range(ITERS - 1 - pairs):
        cur[1] = stepped(cur[1]).astype(bf16)
    here = cur[1]
    poly = poly_of(here)
    for i in range(PIECES):
        cols = slice(i * COLS // PIECES, (i + 1) * COLS // PIECES)
        part = here[:, cols]
        write(1, 1 + i, cols, coef_a * part.astype(f32) + jnp.dot(poly, part, preferred_element_type=f32))
    for copy in copies:
        copy.wait()


def newton(x1, y0, momentum_out):
    vmem = pl.BlockSpec(memory_space=pltpu.VMEM)
    return pl.pallas_call(
        newton_kernel,
        name="newton_schulz",
        out_shape=(jax.ShapeDtypeStruct((MATS, ROWS, COLS), bf16), jax.ShapeDtypeStruct((OWN, MATS, COLS), f32)),
        in_specs=[vmem, vmem, vmem],
        out_specs=(pl.BlockSpec(memory_space=pltpu.HBM), vmem),
        scratch_shapes=[pltpu.VMEM((MATS, ROWS, COLS), bf16), pltpu.VMEM((MATS, ROWS, ROWS), bf16),
                        pltpu.SemaphoreType.DMA((1 + PIECES,))],
        compiler_params=pltpu.CompilerParams(vmem_limit_bytes=40 << 20),
        cost_estimate=pl.CostEstimate(flops=4_300_000_000, bytes_accessed=3_200_000, transcendentals=0),
    )(x1, y0, momentum_out)


def shards(partials, momentum):
    parts = partials.reshape(MATS, NX, NYH, SLAB, COLS)
    old = jnp.transpose(momentum[0], (1, 0, 2))
    update, momentum_out = newton(*comm(parts, old))
    return update[None], jnp.transpose(momentum_out, (1, 0, 2))[None]


def solution(mesh):
    in_specs = (P("group", "dp", None, None, None), P("group", None, "dp", None))
    out_specs = (P("group", None, None, None), P("group", None, "dp", None))
    return jax.shard_map(shards, mesh=mesh, in_specs=in_specs, out_specs=out_specs, check_vma=False)
```
